32 devices in a mesh: groups: 2 (over y), slab: 8 (over z, x), trans: 2 (over core).
Axes of the slice: x: 2, y: 2, z: 4, core: 2. Of those that a mesh axis runs over, the one named last changes fastest.
Arguments:
- volume: float32 [2048, 2048], P(('groups', 'slab'), 'trans'), parts along dimension 0, may hold values from -6 to 6
- col_weight: float32 [2048, 2048], P(('groups', 'slab'), 'trans'), parts along dimension 0, may hold values from 0.5 to 4
- foot_pos: float32 [4, 2048], P(None, 'trans'), may hold values from 0 to 1024
- foot_width: float32 [4, 2048], P(None, 'trans'), may hold values from 1 to 4
- measured: float32 [8, 8, 1024], P(('groups', 'trans'), 'slab'), parts along dimension 0, may hold values from -12 to 12
- row_weight: float32 [8, 8, 1024], P(('groups', 'trans'), 'slab'), parts along dimension 0, may hold values from 0.1 to 1
- row_tiles: bfloat16 [128, 2, 128], P(('groups', 'slab')), parts along dimension 0, may hold values from -0.5 to 0.5
- tile_view_index: int32 [128], P(('groups', 'slab')), parts along dimension 0, may hold values from 0 to 3, as said below
- tile_block: int32 [128], P(('groups', 'slab')), parts along dimension 0, may hold values from 0 to 3, as said below
- tile_count: int32 [16], P(('groups', 'slab')), parts along dimension 0, may hold values from 4 to 8, as said below
Outputs:
- updated: float32 [2048, 2048], P(('groups', 'slab'), 'trans'), parts along dimension 0
- residual: bfloat16 [8, 8, 1024], P(('groups', 'trans'), 'slab'), parts along dimension 0
The draws below stay inside these ranges and needn't reach their ends.
There are 2 independent parts, one for each index of `groups`. The reference program is written for one: setup_inputs(seed, part) draws one part's arguments, and reference() takes and returns one part's arrays. A program takes and returns all parts, laid end to end along the dimension named above; an argument that names none is the same for every part. Nothing has to cross between parts.
Inputs may be any that keep to these rules, and one draw needn't show every extreme that they name: `tile_count`: some slab index has exactly 8 live slots in every draw. `tile_view_index`: slots that are not live hold 0. `tile_block`: slots that are not live hold 0.
All inputs are finite; a program needn't handle non-finite values.
Results may differ from the reference program's by a relative error of at most 0.009.
Values may be sent and summed in bfloat16 or wider, within the bound.
No kernel may reach another device: no remote copies, remote signals or barrier semaphores. Data moves between devices by JAX's collectives and lax.ppermute only.
A program may use at most 64 MiB of HBM per device.

```python
import math
import jax
import jax.numpy as jnp
from jax import lax

ZB = 128
DC = 1024
NV = 4
RB = 2
MAXT = 8
NZ = 1024
NT = 2048
DR = 8
NRB = 4
N_SLAB = 8


def fullest_index(key):
    return jax.random.randint(jax.random.fold_in(key, 12), (), 0, N_SLAB)


def slot_counts(key):
    base_key = jax.random.fold_in(key, 11)
    counts = jax.random.randint(base_key, (N_SLAB,), MAXT // 2, MAXT + 1)
    fullest = fullest_index(key)
    return jnp.where(jnp.arange(N_SLAB) == fullest, MAXT, counts).astype(jnp.int32)


def draw_tile_count(key, part):
    return slot_counts(key)


def draw_tile_view_index(key, part):
    counts = slot_counts(key)
    key = jax.random.fold_in(key, 3)
    slots = jnp.arange(N_SLAB * MAXT)
    owner = slots // MAXT
    offsets = jax.random.randint(key, (N_SLAB,), 0, NV)
    view_ids = (slots % MAXT + offsets[owner]) % NV
    return jnp.where(slots % MAXT < counts[owner], view_ids, 0).astype(jnp.int32)


def draw_tile_block(key, part):
    counts = slot_counts(key)
    fullest = fullest_index(key)
    key = jax.random.fold_in(key, 5)
    slots = jnp.arange(N_SLAB * MAXT)
    owner = slots // MAXT
    block_ids = jax.random.randint(key, (N_SLAB * MAXT,), 0, NRB)
    block_ids = jnp.where(slots == fullest * MAXT, NRB - 1, block_ids)
    block_ids = jnp.where(slots == fullest * MAXT + 1, 0, block_ids)
    return jnp.where(slots % MAXT < counts[owner], block_ids, 0).astype(jnp.int32)


def block_levels(key, shape, cuts, low, top_value):
    level, own = 1.0, jax.random.fold_in(key, 6)
    for dim, shards_of in cuts:
        heights = jnp.exp(jax.random.uniform(jax.random.fold_in(own, dim), (shards_of,), jnp.float32, low / len(cuts), top_value / len(cuts)))
        level = level * jnp.repeat(heights, shape[dim] // shards_of).reshape([-1 if axis == dim else 1 for axis in range(len(shape))])
    return level


def noise(key, extent, spread, reach, shards=(), dtype=jnp.bfloat16):
    gain = block_levels(key, extent, shards, -0.22, 0.18) if shards else 1.0
    array = jax.random.normal(key, extent, jnp.float32) * spread * gain
    return jnp.minimum(jnp.maximum(array, -reach), reach).astype(dtype)


def setup_inputs(seed: int = 0, part: int = 0) -> dict:
    key_list = jax.random.split(jax.random.key(seed), 11)
    part_splits = jax.random.split(jax.random.fold_in(key_list[10], part), 11)
    return {
        "volume": noise(part_splits[0], (NZ, NT), 1.0, 6.0, ((0, 8), (1, 2)), jnp.float32),
        "col_weight": jnp.clip(jnp.exp(math.log(4.0) - 2.0794415 * jax.random.uniform(part_splits[1], (NZ, NT), jnp.float32) ** block_levels(part_splits[1], (NZ, NT), ((0, 8), (1, 2)), -0.2, 0.2)), 0.5, 4.0),
        "foot_pos": jnp.clip(1024.0 * jax.random.uniform(key_list[2], (NV, NT), jnp.float32) ** block_levels(key_list[2], (NV, NT), ((1, 2),), -0.2, 0.2), 0.0, 1024.0),
        "foot_width": jnp.clip(jnp.exp(math.log(4.0) - 1.3862944 * jax.random.uniform(key_list[3], (NV, NT), jnp.float32) ** block_levels(key_list[3], (NV, NT), ((1, 2),), -0.2, 0.2)), 1.0, 4.0),
        "measured": noise(part_splits[4], (NV, DR, DC), 2.0, 12.0, ((0, 2), (1, 8)), jnp.float32),
        "row_weight": jnp.clip(jnp.exp(math.log(1.0) - 2.3025851 * jax.random.uniform(part_splits[5], (NV, DR, DC), jnp.float32) ** block_levels(part_splits[5], (NV, DR, DC), ((0, 2), (1, 8)), -0.2, 0.2)), 0.1, 1.0),
        "row_tiles": noise(part_splits[6], (N_SLAB * MAXT, RB, ZB), ZB ** -0.5, 0.5, ((0, 8),)),
        "tile_view_index": draw_tile_view_index(jax.random.fold_in(jax.random.fold_in(key_list[10], part), 71), part),
        "tile_block": draw_tile_block(jax.random.fold_in(jax.random.fold_in(key_list[10], part), 71), part),
        "tile_count": draw_tile_count(jax.random.fold_in(jax.random.fold_in(key_list[10], part), 71), part),
    }


def footprints(foot_pos, foot_width, det_cols):
    det_coord = jnp.arange(det_cols).astype(jnp.float32) + 0.5
    distance = jnp.abs(det_coord[None, None, :] - foot_pos[:, :, None]) / foot_width[:, :, None]
    return jnp.maximum(0.0, 1.0 - distance).astype(jnp.bfloat16)


def reference(volume, col_weight, foot_pos, foot_width, measured, row_weight, row_tiles, tile_view_index, tile_block, tile_count):
    footprint = footprints(foot_pos, foot_width, DC)
    flat_vol = volume.astype(jnp.bfloat16)
    vox_lines = jnp.stack([jnp.dot(flat_vol, footprint[view_idx], preferred_element_type=jnp.float32) for view_idx in range(NV)]).astype(jnp.bfloat16)
    zero_idx = jnp.zeros((), jnp.int32)

    def slot_info(tile_idx):
        tile_idx = jnp.asarray(tile_idx).astype(jnp.int32)
        slab_idx = (tile_idx // MAXT).astype(jnp.int32)
        is_live = ((tile_idx % MAXT) < tile_count[slab_idx]).astype(jnp.float32)
        view_id = tile_view_index[tile_idx].astype(jnp.int32)
        block_id = tile_block[tile_idx].astype(jnp.int32)
        return tile_idx, slab_idx, is_live, view_id, block_id

    def add_tile(tile_idx, running):
        tile_idx, slab_idx, is_live, view_id, block_id = slot_info(tile_idx)
        vox_block = lax.dynamic_slice(vox_lines, (view_id, slab_idx * ZB, zero_idx), (1, ZB, DC))[0]
        tile_term = jnp.dot(row_tiles[tile_idx], vox_block, preferred_element_type=jnp.float32) * is_live
        current = lax.dynamic_slice(running, (view_id, block_id * RB, zero_idx), (1, RB, DC))
        return lax.dynamic_update_slice(running, current + tile_term[None], (view_id, block_id * RB, zero_idx))

    projected = lax.fori_loop(0, N_SLAB * MAXT, add_tile, jnp.zeros((NV, DR, DC), jnp.float32))
    residual = ((measured - projected) * row_weight).astype(jnp.bfloat16)

    def back_tile(tile_idx, running):
        tile_idx, slab_idx, is_live, view_id, block_id = slot_info(tile_idx)
        res_block = lax.dynamic_slice(residual, (view_id, block_id * RB, zero_idx), (1, RB, DC))[0]
        tile_term = jnp.dot(row_tiles[tile_idx].T, res_block, preferred_element_type=jnp.float32) * is_live
        current = lax.dynamic_slice(running, (view_id, slab_idx * ZB, zero_idx), (1, ZB, DC))
        return lax.dynamic_update_slice(running, current + tile_term[None], (view_id, slab_idx * ZB, zero_idx))

    backprojected_totals = lax.fori_loop(0, N_SLAB * MAXT, back_tile, jnp.zeros((NV, NZ, DC), jnp.float32)).astype(jnp.bfloat16)
    gradient = jnp.zeros((NZ, NT), jnp.float32)
    for view_idx in range(NV):
        gradient = gradient + jnp.dot(backprojected_totals[view_idx], footprint[view_idx].T, preferred_element_type=jnp.float32)
    updated = volume + 0.9 * col_weight * gradient
    return updated, residual
```

```python
import functools

import jax
import jax.numpy as jnp
from jax import lax
from jax.experimental import pallas as pl
from jax.experimental.pallas import tpu as pltpu
from jax.sharding import PartitionSpec as P

LANES = 128
WINDOW = 144
F32 = jnp.float32
BF16 = jnp.bfloat16


def segment_of(pos, width, n_seg):
    first = jnp.floor((pos - width - 0.5) * (1.0 / LANES))
    return jnp.clip(first, 0.0, n_seg - 1.0)


def segment_masks(pos_ref, wid_ref, mask_ref):
    n_views, cols = pos_ref.shape
    n_seg = mask_ref.shape[1]
    seg_ids = lax.broadcasted_iota(jnp.int32, (n_seg, cols), 0).astype(F32)
    for v in range(n_views):
        seg = segment_of(pos_ref[v : v + 1, :], wid_ref[v : v + 1, :], n_seg)
        mask_ref[v] = (seg_ids == seg).astype(F32)


def repeated_tiles(tiles_ref, count_ref, n_seg):
    n_slots, tile_rows, depth = tiles_ref.shape
    tiles = tiles_ref[...].astype(F32)
    rows = []
    for s in range(n_slots):
        live = (s < count_ref[0]).astype(F32)
        for r in range(tile_rows):
            rows.append(jnp.broadcast_to(tiles[s, r : r + 1, :] * live, (n_seg, depth)))
    return jnp.concatenate(rows, axis=0).astype(BF16)


def line_of(detector_row, view, n_views, own_rows):
    owner = detector_row // own_rows
    return (owner * n_views + view) * own_rows + detector_row % own_rows


def project_kernel(
    view_ref, block_ref, count_ref, place_ref, vol_ref, pos_ref, wid_ref, meas_ref, rw_ref, tiles_ref,
    sum_ref, send_ref, win_ref, mask_ref, terms_ref,
):
    n_views, cols = pos_ref.shape
    n_seg = mask_ref.shape[1]
    n_slots, tile_rows, _ = tiles_ref.shape
    shared_views, own_rows, _ = meas_ref.shape
    slab, trans = place_ref[0], place_ref[1]
    slot_rows = tile_rows * n_seg
    lines = sum_ref.shape[0] // n_seg - n_views * own_rows
    segment_masks(pos_ref, wid_ref, mask_ref)
    offsets = lax.broadcasted_iota(jnp.int32, (WINDOW, cols), 0).astype(F32)
    for v in range(n_views):
        pos, wid = pos_ref[v : v + 1, :], wid_ref[v : v + 1, :]
        start = segment_of(pos, wid, n_seg) * LANES + 0.5 - pos
        distance = jnp.abs(offsets + start) * (1.0 / wid)
        win_ref[v] = jnp.maximum(0.0, 1.0 - distance).astype(BF16)
    tiles = repeated_tiles(tiles_ref, count_ref, n_seg)
    rows = jnp.dot(tiles, vol_ref[...].astype(BF16), preferred_element_type=F32)
    terms_ref[...] = jnp.zeros_like(terms_ref)
    for s in range(n_slots):
        view = view_ref[s]
        mask = mask_ref[view]
        spread = rows[s * slot_rows : (s + 1) * slot_rows] * jnp.concatenate([mask] * tile_rows, axis=0)
        terms_ref[s * slot_rows : (s + 1) * slot_rows, :WINDOW] = lax.dot_general(
            spread.astype(BF16), win_ref[view], (((1,), (1,)), ((), ())), preferred_element_type=F32
        )
    over = pltpu.roll(terms_ref[:, LANES:], 1, 0)
    row_ids = lax.broadcasted_iota(jnp.int32, over.shape, 0)
    totals = terms_ref[:, :LANES] + jnp.where(row_ids % n_seg == 0, 0.0, over)
    sum_ref[...] = jnp.zeros_like(sum_ref)

    def place(line):
        return pl.ds(pl.multiple_of(line * n_seg, n_seg), n_seg)

    for s in range(n_slots):
        for r in range(tile_rows):
            k = (s * tile_rows + r) * n_seg
            at = place(line_of(block_ref[s] * tile_rows + r, view_ref[s], n_views, own_rows))
            sum_ref[at, :] = sum_ref[at, :] + totals[k : k + n_seg]
    for i in range(shared_views):
        view = trans * shared_views + i
        for j in range(own_rows):
            at = place((slab * n_views + view) * own_rows + j)
            sum_ref[at, :] = sum_ref[at, :] - folded(meas_ref, i, j, n_seg)
            sum_ref[place(lines + view * own_rows + j), :] = folded(rw_ref, i, j, n_seg)
    send_ref[...] = sum_ref[...].astype(BF16)


def folded(ref, i, j, n_seg):
    return jnp.concatenate([ref[i, j : j + 1, a * LANES : (a + 1) * LANES] for a in range(n_seg)], axis=0)


def update_kernel(
    view_ref, block_ref, count_ref, place_ref, vol_ref, cw_ref, pos_ref, wid_ref, tiles_ref, win_ref, res_ref, got_ref,
    upd_ref, out_ref, mask_ref, val_ref, near_ref, back_ref,
):
    n_views, cols = pos_ref.shape
    n_seg = mask_ref.shape[1]
    n_slots, tile_rows, _ = tiles_ref.shape
    shared_views, own_rows, _ = out_ref.shape
    slab, trans = place_ref[0], place_ref[1]
    slot_rows = tile_rows * n_seg
    segment_masks(pos_ref, wid_ref, mask_ref)
    tiles = repeated_tiles(tiles_ref, count_ref, n_seg)
    val_ref[...] = jnp.where(trans == 0, got_ref[...].astype(F32), res_ref[...].astype(F32))

    def taken(line):
        return val_ref[pl.ds(pl.multiple_of(line * n_seg, n_seg), n_seg), :]

    seg_ids = lax.broadcasted_iota(jnp.int32, (n_seg, LANES), 0)
    for s in range(n_slots):
        for r in range(tile_rows):
            k = (s * tile_rows + r) * n_seg
            line = taken(line_of(block_ref[s] * tile_rows + r, view_ref[s], n_views, own_rows))
            near_ref[k : k + n_seg, :LANES] = line
            near_ref[k : k + n_seg, LANES:] = jnp.where(seg_ids == n_seg - 1, 0.0, pltpu.roll(line, n_seg - 1, 0))
    near = near_ref[:, :WINDOW].astype(BF16)
    for s in range(n_slots):
        view = view_ref[s]
        mask = mask_ref[view]
        part = jnp.dot(near[s * slot_rows : (s + 1) * slot_rows], win_ref[view], preferred_element_type=F32)
        back_ref[s * slot_rows : (s + 1) * slot_rows, :] = (part * jnp.concatenate([mask] * tile_rows, axis=0)).astype(BF16)
    gradient = lax.dot_general(tiles, back_ref[...], (((0,), (0,)), ((), ())), preferred_element_type=F32)
    upd_ref[...] = vol_ref[...] + 0.9 * cw_ref[...] * gradient
    for i in range(shared_views):
        for j in range(own_rows):
            line = taken((slab * n_views + trans * shared_views + i) * own_rows + j).astype(BF16)
            for a in range(n_seg):
                out_ref[i, j : j + 1, a * LANES : (a + 1) * LANES] = line[a : a + 1]


def body(
    volume, col_weight, foot_pos, foot_width, measured, row_weight, row_tiles, tile_view_index, tile_block, tile_count
):
    n_views = foot_pos.shape[0]
    shared_views, own_rows, det_cols = measured.shape
    n_slots, tile_rows, depth = row_tiles.shape
    n_slab, n_trans = lax.axis_size("slab"), lax.axis_size("trans")
    n_seg = det_cols // LANES
    cols = volume.shape[1]
    lines = n_slab * n_views * own_rows
    own_lines = n_views * own_rows
    all_rows = n_slots * tile_rows * n_seg
    slab, trans = lax.axis_index("slab"), lax.axis_index("trans")
    place = jnp.stack([slab, trans]).astype(jnp.int32)
    smem, vmem = pl.BlockSpec(memory_space=pltpu.SMEM), pl.BlockSpec(memory_space=pltpu.VMEM)
    params = pltpu.CompilerParams(vmem_limit_bytes=32 * 1024 * 1024)
    sent = ((lines + own_lines) * n_seg, LANES)
    sums, first, windows = pl.pallas_call(
        project_kernel,
        out_shape=(
            jax.ShapeDtypeStruct(sent, F32),
            jax.ShapeDtypeStruct(sent, BF16),
            jax.ShapeDtypeStruct((n_views, WINDOW, cols), BF16),
        ),
        in_specs=[smem] * 4 + [vmem] * 6,
        out_specs=(vmem,) * 3,
        scratch_shapes=[pltpu.VMEM((n_views, n_seg, cols), F32), pltpu.VMEM((all_rows, 2 * LANES), F32)],
        compiler_params=params,
        name="project",
    )(tile_view_index, tile_block, tile_count, place, volume, foot_pos, foot_width, measured, row_weight, row_tiles)
    sums = sums + lax.ppermute(first, "trans", [(0, 1)]).astype(F32)
    partial, weights = sums[: lines * n_seg], sums[lines * n_seg :].astype(BF16)
    step = 1
    while step < n_slab:
        pairs = [(i * n_trans + 1, (i ^ step) * n_trans + 1) for i in range(n_slab)]
        got = lax.ppermute(jnp.concatenate([partial.astype(BF16), weights], axis=0), ("slab", "trans"), pairs)
        partial = partial + got[: lines * n_seg].astype(F32)
        theirs = got[lines * n_seg :]
        upper = (slab & step) != 0
        weights = jnp.concatenate([jnp.where(upper, theirs, weights), jnp.where(upper, weights, theirs)], axis=0)
        step *= 2
    residual_lines = (-partial * weights.astype(F32)).astype(BF16)
    other = lax.ppermute(residual_lines, "trans", [(1, 0)])
    return pl.pallas_call(
        update_kernel,
        out_shape=(
            jax.ShapeDtypeStruct(volume.shape, F32),
            jax.ShapeDtypeStruct(measured.shape, BF16),
        ),
        in_specs=[smem] * 4 + [vmem] * 8,
        out_specs=(vmem,) * 2,
        scratch_shapes=[
            pltpu.VMEM((n_views, n_seg, cols), F32),
            pltpu.VMEM((lines * n_seg, LANES), F32),
            pltpu.VMEM((all_rows, 2 * LANES), F32),
            pltpu.VMEM((all_rows, cols), BF16),
        ],
        compiler_params=params,
        name="update",
    )(
        tile_view_index, tile_block, tile_count, place, volume, col_weight, foot_pos, foot_width, row_tiles, windows,
        residual_lines, other,
    )


def solution(mesh):
    in_specs = (
        P(("groups", "slab"), "trans"),
        P(("groups", "slab"), "trans"),
        P(None, "trans"),
        P(None, "trans"),
        P(("groups", "trans"), "slab", None),
        P(("groups", "trans"), "slab", None),
        P(("groups", "slab"), None, None),
        P(("groups", "slab")),
        P(("groups", "slab")),
        P(("groups", "slab")),
    )
    out_specs = (P(("groups", "slab"), "trans"), P(("groups", "trans"), "slab", None))
    return jax.shard_map(body, mesh=mesh, in_specs=in_specs, out_specs=out_specs, check_vma=False)
```

```python
import jax
import jax.numpy as jnp
from jax import lax
from jax.experimental import pallas as pl
from jax.experimental.pallas import tpu as pltpu
from jax.sharding import PartitionSpec as P

LANES = 128
WINDOW = 144
F32 = jnp.float32
BF16 = jnp.bfloat16


def parity(index):
    for shift in (8, 4, 2, 1):
        index = index ^ (index >> shift)
    return index & 1


def my_place():
    slab, trans = lax.axis_index("slab"), lax.axis_index("trans")
    return slab, trans, trans ^ parity(slab)


def segment_of(pos, width, n_seg):
    first = jnp.floor((pos - width - 0.5) * (1.0 / LANES))
    return jnp.clip(first, 0.0, n_seg - 1.0)


def repeated_tiles(tiles_ref, count_ref, n_seg):
    n_slots, tile_rows, depth = tiles_ref.shape
    tiles = tiles_ref[...].astype(F32)
    rows = []
    for s in range(n_slots):
        live = (s < count_ref[0]).astype(F32)
        for r in range(tile_rows):
            rows.append(jnp.broadcast_to(tiles[s, r : r + 1, :] * live, (n_seg, depth)))
    return jnp.concatenate(rows, axis=0).astype(BF16)


def line_of(detector_row, view, shared_views, own_rows, half_lines):
    owner = detector_row // own_rows
    inside = (owner * shared_views + view % shared_views) * own_rows + detector_row % own_rows
    return (view // shared_views) * half_lines + inside


def rows_of(line, n_seg):
    return pl.ds(pl.multiple_of(line * n_seg, n_seg), n_seg)


def folded(ref, i, j, n_seg):
    return jnp.concatenate([ref[i, j : j + 1, a * LANES : (a + 1) * LANES] for a in range(n_seg)], axis=0)


def project_kernel(
    view_hbm, block_hbm, vol_hbm, pos_hbm, wid_hbm, meas_hbm, rw_hbm, tiles_hbm, count_ref,
    keep_ref, send_ref, win_ref, mask_ref, wide_ref,
    view_ref, block_ref, vol_ref, pos_ref, wid_ref, meas_ref, rw_ref, tiles_ref, sum_ref, terms_ref, sems,
):
    inputs = (pos_hbm, wid_hbm, vol_hbm, tiles_hbm, view_hbm, block_hbm, meas_hbm, rw_hbm)
    holders = (pos_ref, wid_ref, vol_ref, tiles_ref, view_ref, block_ref, meas_ref, rw_ref)
    copies = [pltpu.make_async_copy(a, b, sems.at[i]) for i, (a, b) in enumerate(zip(inputs, holders))]
    for copy in copies:
        copy.start()
    n_views, cols = pos_ref.shape
    n_slots, tile_rows, _ = tiles_ref.shape
    shared_views, own_rows, det_cols = meas_ref.shape
    n_seg = det_cols // LANES
    slab, trans, half = my_place()
    slot_rows = tile_rows * n_seg
    half_rows = keep_ref.shape[0]
    half_lines = half_rows // n_seg
    sum_ref[...] = jnp.zeros_like(sum_ref)
    terms_ref[:, LANES:] = jnp.zeros((terms_ref.shape[0], LANES), F32)
    seg_ids = lax.broadcasted_iota(jnp.int32, (n_seg, cols), 0).astype(F32)
    offsets = lax.broadcasted_iota(jnp.int32, (WINDOW, cols), 0).astype(F32)
    copies[0].wait()
    copies[1].wait()
    for v in range(n_views):
        pos, wid = pos_ref[v : v + 1, :], wid_ref[v : v + 1, :]
        seg = segment_of(pos, wid, n_seg)
        mask_ref[v] = (seg_ids == seg).astype(F32)
        distance = jnp.abs(offsets + (seg * LANES + 0.5 - pos)) * (1.0 / wid)
        win_ref[v] = jnp.maximum(0.0, 1.0 - distance).astype(BF16)
    for copy in copies[2:]:
        copy.wait()
    tiles = repeated_tiles(tiles_ref, count_ref, n_seg)
    wide_ref[...] = tiles
    rows = jnp.dot(tiles, vol_ref[...].astype(BF16), preferred_element_type=F32)
    for s in range(n_slots):
        view = view_ref[s]
        mask = mask_ref[view]
        spread = rows[s * slot_rows : (s + 1) * slot_rows] * jnp.concatenate([mask] * tile_rows, axis=0)
        terms_ref[s * slot_rows : (s + 1) * slot_rows, :WINDOW] = lax.dot_general(
            spread.astype(BF16), win_ref[view], (((1,), (1,)), ((), ())), preferred_element_type=F32
        )
    over = pltpu.roll(terms_ref[:, LANES:], 1, 0)
    row_ids = lax.broadcasted_iota(jnp.int32, over.shape, 0)
    totals = terms_ref[:, :LANES] + jnp.where(row_ids % n_seg == 0, 0.0, over)
    for s in range(n_slots):
        for r in range(tile_rows):
            k = (s * tile_rows + r) * n_seg
            line = line_of(block_ref[s] * tile_rows + r, view_ref[s], shared_views, own_rows, half_lines)
            at = rows_of(line, n_seg)
            sum_ref[at, :] = sum_ref[at, :] + totals[k : k + n_seg]
    for i in range(shared_views):
        for j in range(own_rows):
            line = line_of(slab * own_rows + j, trans * shared_views + i, shared_views, own_rows, half_lines)
            at = rows_of(line, n_seg)
            sum_ref[at, :] = sum_ref[at, :] - folded(meas_ref, i, j, n_seg)
    keep_ref[...] = sum_ref[pl.ds(pl.multiple_of(half * half_rows, n_seg), half_rows), :]
    away = sum_ref[pl.ds(pl.multiple_of((1 - half) * half_rows, n_seg), half_rows), :]
    weights = [folded(rw_ref, i, j, n_seg) for i in range(shared_views) for j in range(own_rows)]
    send_ref[...] = jnp.concatenate([away] + weights, axis=0).astype(BF16)


def update_kernel(
    view_ref, block_ref, vol_ref, cw_ref, wide_ref, win_ref, mask_ref, res_ref, got_ref,
    upd_hbm, out_ref,
    val_ref, near_ref, back_ref, upd_ref, sems,
):
    n_views, n_seg, cols = mask_ref.shape
    n_slots = view_ref.shape[0]
    shared_views, own_rows, _ = out_ref.shape
    tile_rows = near_ref.shape[0] // (n_slots * n_seg)
    slab, trans, half = my_place()
    slot_rows = tile_rows * n_seg
    half_rows = res_ref.shape[0]
    half_lines = half_rows // n_seg
    val_ref[pl.ds(pl.multiple_of(half * half_rows, n_seg), half_rows), :] = res_ref[...].astype(F32)
    val_ref[pl.ds(pl.multiple_of((1 - half) * half_rows, n_seg), half_rows), :] = got_ref[...].astype(F32)

    def taken(detector_row, view):
        return val_ref[rows_of(line_of(detector_row, view, shared_views, own_rows, half_lines), n_seg), :]

    seg_ids = lax.broadcasted_iota(jnp.int32, (n_seg, LANES), 0)
    for s in range(n_slots):
        for r in range(tile_rows):
            k = (s * tile_rows + r) * n_seg
            line = taken(block_ref[s] * tile_rows + r, view_ref[s])
            near_ref[k : k + n_seg, :LANES] = line
            near_ref[k : k + n_seg, LANES:] = jnp.where(seg_ids == n_seg - 1, 0.0, pltpu.roll(line, n_seg - 1, 0))
    near = near_ref[:, :WINDOW].astype(BF16)
    for s in range(n_slots):
        view = view_ref[s]
        mask = mask_ref[view]
        part = jnp.dot(near[s * slot_rows : (s + 1) * slot_rows], win_ref[view], preferred_element_type=F32)
        back_ref[s * slot_rows : (s + 1) * slot_rows, :] = (part * jnp.concatenate([mask] * tile_rows, axis=0)).astype(BF16)
    n_parts = sems.shape[0]
    width = cols // n_parts
    copies = []
    for p in range(n_parts):
        at = slice(p * width, (p + 1) * width)
        gradient = lax.dot_general(
            wide_ref[...], back_ref[:, at], (((0,), (0,)), ((), ())), preferred_element_type=F32
        )
        upd_ref[:, at] = vol_ref[:, at] + 0.9 * cw_ref[:, at] * gradient
        copies.append(pltpu.make_async_copy(upd_ref.at[:, at], upd_hbm.at[:, at], sems.at[p]))
        copies[-1].start()
    for i in range(shared_views):
        for j in range(own_rows):
            line = taken(slab * own_rows + j, trans * shared_views + i).astype(BF16)
            for a in range(n_seg):
                out_ref[i, j : j + 1, a * LANES : (a + 1) * LANES] = line[a : a + 1]
    for copy in copies:
        copy.wait()


def exchange(array, slab_mask, n_slab, n_trans):
    pairs = []
    for i in range(n_slab):
        for k in range(n_trans):
            pairs.append((i * n_trans + k, (i ^ slab_mask) * n_trans + (k ^ parity(slab_mask))))
    return lax.ppermute(array, ("slab", "trans"), pairs)


def in_order(blocks, index):
    step = 1
    while step < len(blocks):
        odd = (index & step) != 0
        blocks = [jnp.where(odd, blocks[q ^ step], blocks[q]) for q in range(len(blocks))]
        step *= 2
    return blocks


def body(
    volume, col_weight, foot_pos, foot_width, measured, row_weight, row_tiles, tile_view_index, tile_block, tile_count
):
    n_views = foot_pos.shape[0]
    shared_views, own_rows, det_cols = measured.shape
    n_slots, tile_rows, depth = row_tiles.shape
    n_slab, n_trans = lax.axis_size("slab"), lax.axis_size("trans")
    assert n_trans == 2 and n_slab & (n_slab - 1) == 0
    n_seg = det_cols // LANES
    cols = volume.shape[1]
    half_rows = n_slab * shared_views * own_rows * n_seg
    own = shared_views * own_rows * n_seg
    all_rows = n_slots * tile_rows * n_seg
    smem, vmem = pl.BlockSpec(memory_space=pltpu.SMEM), pl.BlockSpec(memory_space=pltpu.VMEM)
    hbm = pl.BlockSpec(memory_space=pltpu.HBM)
    params = pltpu.CompilerParams(vmem_limit_bytes=32 * 1024 * 1024)
    keep, send, windows, masks, wide = pl.pallas_call(
        project_kernel,
        out_shape=(
            jax.ShapeDtypeStruct((half_rows, LANES), F32),
            jax.ShapeDtypeStruct((half_rows + own, LANES), BF16),
            jax.ShapeDtypeStruct((n_views, WINDOW, cols), BF16),
            jax.ShapeDtypeStruct((n_views, n_seg, cols), F32),
            jax.ShapeDtypeStruct((all_rows, depth), BF16),
        ),
        in_specs=[hbm] * 8 + [smem],
        out_specs=(vmem,) * 5,
        scratch_shapes=[
            pltpu.SMEM(tile_view_index.shape, jnp.int32),
            pltpu.SMEM(tile_block.shape, jnp.int32),
            pltpu.VMEM(volume.shape, F32),
            pltpu.VMEM(foot_pos.shape, F32),
            pltpu.VMEM(foot_width.shape, F32),
            pltpu.VMEM(measured.shape, F32),
            pltpu.VMEM(row_weight.shape, F32),
            pltpu.VMEM(row_tiles.shape, BF16),
            pltpu.VMEM((n_trans * half_rows, LANES), F32),
            pltpu.VMEM((all_rows, 2 * LANES), F32),
            pltpu.SemaphoreType.DMA((8,)),
        ],
        compiler_params=params,
        name="project",
    )(
        *[
            pltpu.with_memory_space_constraint(array, pltpu.HBM)
            for array in (tile_view_index, tile_block, volume, foot_pos, foot_width, measured, row_weight, row_tiles)
        ],
        tile_count,
    )

    slab, trans, half = my_place()
    got = lax.ppermute(send, "trans", [(0, 1), (1, 0)])
    partial = keep + got[:half_rows].astype(F32)
    weights = jnp.where(half == trans, send[half_rows:], got[half_rows:])
    bit = 1
    while bit < n_slab:
        radix = 2 if (n_slab // bit).bit_length() % 2 == 0 else 4
        sent = jnp.concatenate([partial.astype(BF16), weights], axis=0)
        arrived = [exchange(sent, m * bit, n_slab, n_trans) for m in range(1, radix)]
        for other in arrived:
            partial = partial + other[:half_rows].astype(F32)
        blocks = [weights] + [other[half_rows:] for other in arrived]
        weights = jnp.concatenate(in_order(blocks, slab // bit), axis=0)
        bit *= radix
    residual_lines = (-partial * weights.astype(F32)).astype(BF16)
    other_lines = lax.ppermute(residual_lines, "trans", [(0, 1), (1, 0)])

    n_parts = 4
    return pl.pallas_call(
        update_kernel,
        out_shape=(
            jax.ShapeDtypeStruct(volume.shape, F32),
            jax.ShapeDtypeStruct(measured.shape, BF16),
        ),
        in_specs=[smem] * 2 + [vmem] * 7,
        out_specs=(hbm, vmem),
        scratch_shapes=[
            pltpu.VMEM((n_trans * half_rows, LANES), F32),
            pltpu.VMEM((all_rows, 2 * LANES), F32),
            pltpu.VMEM((all_rows, cols), BF16),
            pltpu.VMEM(volume.shape, F32),
            pltpu.SemaphoreType.DMA((n_parts,)),
        ],
        compiler_params=params,
        name="update",
    )(tile_view_index, tile_block, volume, col_weight, wide, windows, masks, residual_lines, other_lines)


def solution(mesh):
    in_specs = (
        P(("groups", "slab"), "trans"),
        P(("groups", "slab"), "trans"),
        P(None, "trans"),
        P(None, "trans"),
        P(("groups", "trans"), "slab", None),
        P(("groups", "trans"), "slab", None),
        P(("groups", "slab"), None, None),
        P(("groups", "slab")),
        P(("groups", "slab")),
        P(("groups", "slab")),
    )
    out_specs = (P(("groups", "slab"), "trans"), P(("groups", "trans"), "slab", None))
    return jax.shard_map(body, mesh=mesh, in_specs=in_specs, out_specs=out_specs, check_vma=False)
```

```python
import jax
import jax.numpy as jnp
from jax import lax
from jax.experimental import pallas as pl
from jax.experimental.pallas import tpu as pltpu
from jax.sharding import PartitionSpec as P

LANES = 128
WINDOW = 144
GROUP = 8
META = 16
F32 = jnp.float32
BF16 = jnp.bfloat16


def iota(shape, dim):
    return lax.broadcasted_iota(jnp.int32, shape, dim)


def segment_of(pos, width, n_seg):
    first = jnp.floor((pos - width - 0.5) * (1.0 / LANES))
    return jnp.clip(first, 0.0, n_seg - 1.0)


def slot_vector(values, repeat, index):
    result = jnp.full(index.shape, values[0], jnp.int32)
    for s in range(1, len(values)):
        result = jnp.where(index >= s * repeat, values[s], result)
    return result


def slot_lines(view_ref, block_ref, count_ref, index, tile_rows, n_views, own_rows):
    n_slots = view_ref.shape[0]
    view = slot_vector([view_ref[s] for s in range(n_slots)], tile_rows, index)
    block = slot_vector([block_ref[s] for s in range(n_slots)], tile_rows, index)
    detector_row = block * tile_rows + index % tile_rows
    line = (detector_row // own_rows * n_views + view) * own_rows + detector_row % own_rows
    return jnp.where(index // tile_rows < count_ref[0], line, -1)


def project_kernel(
    view_hbm, vol_hbm, pos_hbm, wid_hbm, meas_hbm, rw_hbm, tiles_hbm,
    own_ref, send_ref, win_ref, key_ref, flat_ref,
    view_ref, vol_ref, pos_ref, wid_ref, meas_ref, rw_ref, tiles_ref, spread_ref, sems,
):
    inputs = (pos_hbm, wid_hbm, vol_hbm, tiles_hbm, view_hbm, meas_hbm, rw_hbm)
    holders = (pos_ref, wid_ref, vol_ref, tiles_ref, view_ref, meas_ref, rw_ref)
    copies = [pltpu.make_async_copy(a, b, sems.at[i]) for i, (a, b) in enumerate(zip(inputs, holders))]
    for copy in copies:
        copy.start()
    n_views, cols = pos_ref.shape
    n_slots, tile_rows, _ = tiles_ref.shape
    shared_views, own_rows, det_cols = meas_ref.shape
    n_seg = det_cols // LANES
    slot_rows = n_slots * tile_rows
    own_lines = n_views * own_rows
    trans = lax.axis_index("trans")
    offsets = iota((WINDOW, cols), 0).astype(F32)
    copies[0].wait()
    copies[1].wait()
    segments = []
    for v in range(n_views):
        pos, wid = pos_ref[v : v + 1, :], wid_ref[v : v + 1, :]
        seg = segment_of(pos, wid, n_seg)
        segments.append(seg + float(v * n_seg))
        distance = jnp.abs(offsets + (seg * LANES + 0.5 - pos)) * (1.0 / wid)
        win_ref[v] = jnp.maximum(0.0, 1.0 - distance).astype(BF16)
    for copy in copies[2:]:
        copy.wait()
    views = slot_vector([view_ref[s] for s in range(n_slots)], tile_rows, iota((slot_rows, cols), 0))
    key = jnp.broadcast_to(segments[0], (slot_rows, cols))
    for v in range(1, n_views):
        key = jnp.where(views == v, segments[v], key)
    key_ref[...] = key
    tiles = tiles_ref[...].astype(F32)
    flat = jnp.concatenate([tiles[s, r : r + 1, :] for s in range(n_slots) for r in range(tile_rows)], axis=0)
    flat = flat.astype(BF16)
    flat_ref[...] = flat
    rows = jnp.dot(flat, vol_ref[...].astype(BF16), preferred_element_type=F32)
    sums = jnp.zeros((n_seg * slot_rows, WINDOW), F32)
    for v in range(n_views):
        for a in range(n_seg):
            spread_ref[v, a * slot_rows : (a + 1) * slot_rows, :] = jnp.where(key == v * n_seg + a, rows, 0.0).astype(BF16)
        sums = sums + lax.dot_general(
            spread_ref[v], win_ref[v], (((1,), (1,)), ((), ())), preferred_element_type=F32
        )
    edge = WINDOW - LANES
    own_ref[: n_seg * slot_rows, :] = sums[:, :LANES]
    own_ref[slot_rows : n_seg * slot_rows, :edge] += sums[: (n_seg - 1) * slot_rows, LANES:]
    lines = own_ref.shape[0] // n_seg - slot_rows
    place = iota((lines, det_cols), 0)
    block = jnp.zeros((lines, det_cols), F32)
    for i in range(shared_views):
        for j in range(own_rows):
            at = (trans * shared_views + i) * own_rows + j
            block = jnp.where(place == at, rw_ref[i, j : j + 1, :], block)
            block = jnp.where(place == own_lines + at, meas_ref[i, j : j + 1, :], block)
    for a in range(n_seg):
        at = n_seg * slot_rows + a * lines
        own_ref[at : at + lines, :] = block[:, a * LANES : (a + 1) * LANES]
    send_ref[...] = own_ref[...].astype(BF16)


def join_kernel(view_ref, block_ref, count_ref, own_ref, got_ref, out_ref, *, tile_rows, n_views, own_rows):
    n_rows = own_ref.shape[0]
    out_ref[:n_rows, :] = (own_ref[...] + got_ref[...].astype(F32)).astype(BF16)
    shape = (META, LANES)
    index = iota(shape, 1) % (view_ref.shape[0] * tile_rows)
    line = slot_lines(view_ref, block_ref, count_ref, index, tile_rows, n_views, own_rows)
    part = jnp.where(iota(shape, 0) == 0, line & 127, line >> 7)
    out_ref[n_rows:, :] = part.astype(F32).astype(BF16)


def gather_kernel(*refs, masks, slot_rows, own_lines, n_seg):
    payloads, (part_ref, send_ref, all_ref) = refs[:-3], refs[-3:]
    slab, trans = lax.axis_index("slab"), lax.axis_index("trans")
    lines = part_ref.shape[0] // 2
    depth = all_ref.shape[0]
    n_sources = len(payloads)
    block_lines = (payloads[0].shape[0] - META) // n_seg - slot_rows
    first_block = n_sources * slot_rows
    lane = iota((1, depth), 1)
    sum_line = jnp.full((1, depth), -1, jnp.int32)
    weight_line = sum_line
    if first_block + n_sources * block_lines < depth:
        used = first_block + n_sources * block_lines
        all_ref[used:, :] = jnp.zeros((depth - used, all_ref.shape[1]), F32)
    for j, ref in enumerate(payloads):
        values = ref[...].astype(F32)
        mask = jnp.where(trans == 0, masks[j][0], masks[j][1])
        taken = mask >= 0
        meta = values[n_seg * (slot_rows + block_lines) :]
        line = (meta[0:1, :] + 128.0 * meta[1:2, :]).astype(jnp.int32)
        line = jnp.concatenate([line] * (depth // LANES), axis=1)
        here = (lane >= j * slot_rows) & (lane < (j + 1) * slot_rows)
        sum_line = jnp.where(here & taken, line, sum_line)
        at = first_block + j * block_lines
        inside = lane - at
        base = (slab ^ mask) * own_lines
        weights = (inside >= 0) & (inside < own_lines) & taken
        weight_line = jnp.where(weights, base + inside, weight_line)
        measured = (inside >= own_lines) & (inside < 2 * own_lines) & taken
        sum_line = jnp.where(measured, base + inside - own_lines, sum_line)
        for a in range(n_seg):
            lanes = slice(a * LANES, (a + 1) * LANES)
            all_ref[j * slot_rows : (j + 1) * slot_rows, lanes] = values[a * slot_rows : (a + 1) * slot_rows]
            start = n_seg * slot_rows + a * block_lines
            all_ref[at : at + block_lines, lanes] = values[start : start + block_lines]
    ids = iota((lines, depth), 0)
    sign = jnp.where(lane >= first_block, -1.0, 1.0)
    chosen = jnp.concatenate(
        [jnp.where(ids == sum_line, sign, 0.0), jnp.where(ids == weight_line, 1.0, 0.0)], axis=0
    )
    part = jnp.dot(chosen.astype(BF16), all_ref[...].astype(BF16), preferred_element_type=F32)
    part_ref[...] = part
    send_ref[...] = part.astype(BF16)


def update_kernel(
    view_ref, block_ref, count_ref, vol_ref, cw_ref, flat_ref, win_ref, key_ref, part_ref, got_ref,
    upd_hbm, out_hbm,
    val_ref, near_ref, upd_ref, out_ref, sems, out_sem,
):
    n_views, _, cols = win_ref.shape
    own_rows, shared_views, det_cols = out_ref.shape
    n_seg = det_cols // LANES
    slot_rows = key_ref.shape[0]
    tile_rows = slot_rows // view_ref.shape[0]
    slab, trans = lax.axis_index("slab"), lax.axis_index("trans")
    lines = part_ref.shape[0] // 2
    total = part_ref[...] + got_ref[...].astype(F32)
    residual = (-total[:lines] * total[lines:]).astype(BF16)
    val_ref[...] = residual.astype(F32)
    line = slot_lines(view_ref, block_ref, count_ref, iota((slot_rows, lines), 0), tile_rows, n_views, own_rows)
    chosen = jnp.where(iota((slot_rows, lines), 1) == line, 1.0, 0.0).astype(BF16)
    near = jnp.dot(chosen, residual, preferred_element_type=F32).astype(BF16)
    for a in range(n_seg):
        at = slice(a * slot_rows, (a + 1) * slot_rows)
        near_ref[at, :LANES] = near[:, a * LANES : (a + 1) * LANES]
        if a + 1 < n_seg:
            near_ref[at, LANES:] = near[:, (a + 1) * LANES : (a + 2) * LANES]
        else:
            near_ref[at, LANES:] = jnp.zeros((slot_rows, LANES), BF16)
    n_parts = sems.shape[0]
    width = cols // n_parts
    copies = []
    for p in range(n_parts):
        at = slice(p * width, (p + 1) * width)
        key = key_ref[:, at]
        back = jnp.zeros((slot_rows, width), F32)
        for v in range(n_views):
            part = jnp.dot(near_ref[:, :WINDOW], win_ref[v, :, at], preferred_element_type=F32)
            for a in range(n_seg):
                back = jnp.where(key == v * n_seg + a, part[a * slot_rows : (a + 1) * slot_rows], back)
        gradient = lax.dot_general(
            flat_ref[...], back.astype(BF16), (((0,), (0,)), ((), ())), preferred_element_type=F32
        )
        upd_ref[:, at] = vol_ref[:, at] + 0.9 * cw_ref[:, at] * gradient
        copies.append(pltpu.make_async_copy(upd_ref.at[:, at], upd_hbm.at[:, at], sems.at[p]))
        copies[-1].start()
    for i in range(shared_views):
        for j in range(own_rows):
            line = (slab * n_views + trans * shared_views + i) * own_rows + j
            out_ref[j, i : i + 1, :] = val_ref[pl.ds(line, 1), :].astype(BF16)
    copies.append(pltpu.make_async_copy(out_ref, out_hbm, out_sem))
    copies[-1].start()
    for copy in copies:
        copy.wait()


def exchange(array, masks, n_slab):
    pairs = []
    for i in range(n_slab):
        for k, mask in enumerate(masks):
            pairs.append(((i ^ mask) * len(masks) + k, i * len(masks) + k))
    return lax.ppermute(array, ("slab", "trans"), pairs)


def direct_masks(n_group):
    far = list(range(n_group // 2, n_group))
    near = list(range(1, n_group // 2))
    return [(near[j] if j < len(near) else None, mask) for j, mask in enumerate(far)]


def body(
    volume, col_weight, foot_pos, foot_width, measured, row_weight, row_tiles, tile_view_index, tile_block, tile_count
):
    n_views, cols = foot_pos.shape
    shared_views, own_rows, det_cols = measured.shape
    n_slots, tile_rows, depth = row_tiles.shape
    n_slab, n_trans = lax.axis_size("slab"), lax.axis_size("trans")
    assert n_trans == 2 and n_slab & (n_slab - 1) == 0 and n_slab > 1
    n_seg = det_cols // LANES
    slot_rows = n_slots * tile_rows
    own_lines = n_views * own_rows
    lines = n_slab * own_lines
    block_lines = -(-2 * own_lines // 8) * 8
    first_rows = n_seg * (slot_rows + block_lines)
    smem, vmem = pl.BlockSpec(memory_space=pltpu.SMEM), pl.BlockSpec(memory_space=pltpu.VMEM)
    hbm = pl.BlockSpec(memory_space=pltpu.HBM)
    params = pltpu.CompilerParams(vmem_limit_bytes=32 * 1024 * 1024)
    near = (tile_view_index, volume, foot_pos, foot_width, measured, row_weight, row_tiles)
    own, send, windows, key, flat = pl.pallas_call(
        project_kernel,
        out_shape=(
            jax.ShapeDtypeStruct((first_rows, LANES), F32),
            jax.ShapeDtypeStruct((first_rows, LANES), BF16),
            jax.ShapeDtypeStruct((n_views, WINDOW, cols), BF16),
            jax.ShapeDtypeStruct((slot_rows, cols), F32),
            jax.ShapeDtypeStruct((slot_rows, depth), BF16),
        ),
        in_specs=[hbm] * 7,
        out_specs=(vmem,) * 5,
        scratch_shapes=[
            pltpu.SMEM(tile_view_index.shape, jnp.int32),
            pltpu.VMEM(volume.shape, F32),
            pltpu.VMEM(foot_pos.shape, F32),
            pltpu.VMEM(foot_width.shape, F32),
            pltpu.VMEM(measured.shape, F32),
            pltpu.VMEM(row_weight.shape, F32),
            pltpu.VMEM(row_tiles.shape, BF16),
            pltpu.VMEM((n_views, n_seg * slot_rows, cols), BF16),
            pltpu.SemaphoreType.DMA((7,)),
        ],
        compiler_params=params,
        name="project",
    )(*[pltpu.with_memory_space_constraint(array, pltpu.HBM) for array in near])

    swap = [(0, 1), (1, 0)]
    got = lax.ppermute(send, "trans", swap)
    tile_count, own = lax.optimization_barrier((tile_count, own))

    def join(*args):
        join_kernel(*args, tile_rows=tile_rows, n_views=n_views, own_rows=own_rows)

    payload = pl.pallas_call(
        join,
        out_shape=jax.ShapeDtypeStruct((first_rows + META, LANES), BF16),
        in_specs=[smem] * 3 + [vmem] * 2,
        out_specs=vmem,
        compiler_params=params,
        name="join",
    )(tile_view_index, tile_block, tile_count, own, got)

    n_group = min(GROUP, n_slab)
    steps = direct_masks(n_group)
    arrived = [exchange(payload, (1 if a is None else a, b), n_slab) for a, b in steps]
    masks = [(0, -1)] + [(-1 if a is None else a, b) for a, b in steps]

    def gather(*refs):
        gather_kernel(*refs, masks=masks, slot_rows=slot_rows, own_lines=own_lines, n_seg=n_seg)

    part_shape = (2 * lines, det_cols)
    all_depth = -(-len(masks) * (slot_rows + block_lines) // LANES) * LANES
    part, send = pl.pallas_call(
        gather,
        out_shape=(jax.ShapeDtypeStruct(part_shape, F32), jax.ShapeDtypeStruct(part_shape, BF16)),
        in_specs=[vmem] * len(masks),
        out_specs=(vmem,) * 2,
        scratch_shapes=[pltpu.VMEM((all_depth, det_cols), F32)],
        compiler_params=params,
        name="gather",
    )(payload, *arrived)
    bit = n_group
    while bit < n_slab:
        part = part + exchange(send, (bit, bit), n_slab).astype(F32)
        send = part.astype(BF16)
        bit *= 2
    other = lax.ppermute(send, "trans", swap)

    n_parts = 4
    updated, residual = pl.pallas_call(
        update_kernel,
        out_shape=(
            jax.ShapeDtypeStruct(volume.shape, F32),
            jax.ShapeDtypeStruct((own_rows, shared_views, det_cols), BF16),
        ),
        in_specs=[smem] * 3 + [vmem] * 7,
        out_specs=(hbm, hbm),
        scratch_shapes=[
            pltpu.VMEM((lines, det_cols), F32),
            pltpu.VMEM((n_seg * slot_rows, 2 * LANES), BF16),
            pltpu.VMEM(volume.shape, F32),
            pltpu.VMEM((own_rows, shared_views, det_cols), BF16),
            pltpu.SemaphoreType.DMA((n_parts,)),
            pltpu.SemaphoreType.DMA(()),
        ],
        compiler_params=params,
        name="update",
    )(tile_view_index, tile_block, tile_count, volume, col_weight, flat, windows, key, part, other)
    return updated, jnp.transpose(residual, (1, 0, 2))


def solution(mesh):
    in_specs = (
        P(("groups", "slab"), "trans"),
        P(("groups", "slab"), "trans"),
        P(None, "trans"),
        P(None, "trans"),
        P(("groups", "trans"), "slab", None),
        P(("groups", "trans"), "slab", None),
        P(("groups", "slab"), None, None),
        P(("groups", "slab")),
        P(("groups", "slab")),
        P(("groups", "slab")),
    )
    out_specs = (P(("groups", "slab"), "trans"), P(("groups", "trans"), "slab", None))
    return jax.shard_map(body, mesh=mesh, in_specs=in_specs, out_specs=out_specs, check_vma=False)
```

```python
import jax
import jax.numpy as jnp
from jax import lax
from jax.experimental import pallas as pl
from jax.experimental.pallas import tpu as pltpu
from jax.sharding import PartitionSpec as P

LANES = 128
WINDOW = 144
GROUP = 8
META = 16
F32 = jnp.float32
BF16 = jnp.bfloat16


def iota(shape, dim):
    return lax.broadcasted_iota(jnp.int32, shape, dim)


def segment_of(pos, width, n_seg):
    first = jnp.floor((pos - width - 0.5) * (1.0 / LANES))
    return jnp.clip(first, 0.0, n_seg - 1.0)


def slot_vector(values, repeat, index):
    result = jnp.full(index.shape, values[0], jnp.int32)
    for s in range(1, len(values)):
        result = jnp.where(index >= s * repeat, values[s], result)
    return result


def slot_lines(view_ref, block_ref, tile_rows, n_views, own_rows):
    lines = []
    for s in range(view_ref.shape[0]):
        for r in range(tile_rows):
            detector_row = block_ref[s] * tile_rows + r
            lines.append((detector_row // own_rows * n_views + view_ref[s]) * own_rows + detector_row % own_rows)
    return lines


def project_kernel(
    view_hbm, block_hbm, vol_hbm, pos_hbm, wid_hbm, meas_hbm, rw_hbm, tiles_hbm,
    own_ref, send_ref, win_ref, key_ref, flat_ref, across_ref, down_ref,
    view_ref, block_ref, vol_ref, pos_ref, wid_ref, meas_ref, rw_ref, tiles_ref, spread_ref, sems,
):
    inputs = (pos_hbm, wid_hbm, vol_hbm, tiles_hbm, view_hbm, block_hbm, meas_hbm, rw_hbm)
    holders = (pos_ref, wid_ref, vol_ref, tiles_ref, view_ref, block_ref, meas_ref, rw_ref)
    copies = [pltpu.make_async_copy(a, b, sems.at[i]) for i, (a, b) in enumerate(zip(inputs, holders))]
    for copy in copies:
        copy.start()
    n_views, cols = pos_ref.shape
    n_slots, tile_rows, _ = tiles_ref.shape
    shared_views, own_rows, det_cols = meas_ref.shape
    n_seg = det_cols // LANES
    slot_rows = n_slots * tile_rows
    own_lines = n_views * own_rows
    trans = lax.axis_index("trans")
    offsets = iota((WINDOW, cols), 0).astype(F32)
    copies[0].wait()
    copies[1].wait()
    segments = []
    for v in range(n_views):
        pos, wid = pos_ref[v : v + 1, :], wid_ref[v : v + 1, :]
        seg = segment_of(pos, wid, n_seg)
        segments.append(seg + float(v * n_seg))
        distance = jnp.abs(offsets + (seg * LANES + 0.5 - pos)) * (1.0 / wid)
        win_ref[v] = jnp.maximum(0.0, 1.0 - distance).astype(BF16)
    for copy in copies[2:]:
        copy.wait()
    numbers = slot_lines(view_ref, block_ref, tile_rows, n_views, own_rows)
    across_ref[...] = slot_vector(numbers, 1, iota(across_ref.shape, 1) & (slot_rows - 1))
    down_ref[...] = slot_vector(numbers, 1, iota(down_ref.shape, 0))
    views = slot_vector([view_ref[s] for s in range(n_slots)], tile_rows, iota((slot_rows, cols), 0))
    key = jnp.broadcast_to(segments[0], (slot_rows, cols))
    for v in range(1, n_views):
        key = jnp.where(views == v, segments[v], key)
    key_ref[...] = key
    tiles = tiles_ref[...].astype(F32)
    flat = jnp.concatenate([tiles[s, r : r + 1, :] for s in range(n_slots) for r in range(tile_rows)], axis=0)
    flat = flat.astype(BF16)
    flat_ref[...] = flat
    rows = jnp.dot(flat, vol_ref[...].astype(BF16), preferred_element_type=F32)
    sums = jnp.zeros((n_seg * slot_rows, WINDOW), F32)
    for v in range(n_views):
        for a in range(n_seg):
            spread_ref[v, a * slot_rows : (a + 1) * slot_rows, :] = jnp.where(key == v * n_seg + a, rows, 0.0).astype(BF16)
        sums = sums + lax.dot_general(
            spread_ref[v], win_ref[v], (((1,), (1,)), ((), ())), preferred_element_type=F32
        )
    edge = WINDOW - LANES
    own_ref[: n_seg * slot_rows, :] = sums[:, :LANES]
    own_ref[slot_rows : n_seg * slot_rows, :edge] += sums[: (n_seg - 1) * slot_rows, LANES:]
    lines = own_ref.shape[0] // n_seg - slot_rows
    place = iota((lines, det_cols), 0)
    block = jnp.zeros((lines, det_cols), F32)
    for i in range(shared_views):
        for j in range(own_rows):
            at = (trans * shared_views + i) * own_rows + j
            block = jnp.where(place == at, rw_ref[i, j : j + 1, :], block)
            block = jnp.where(place == own_lines + at, meas_ref[i, j : j + 1, :], block)
    for a in range(n_seg):
        at = n_seg * slot_rows + a * lines
        own_ref[at : at + lines, :] = block[:, a * LANES : (a + 1) * LANES]
    send_ref[...] = own_ref[...].astype(BF16)


def join_kernel(count_ref, across_ref, own_ref, got_ref, out_ref, *, tile_rows, slot_rows):
    n_rows = own_ref.shape[0]
    out_ref[:n_rows, :] = (own_ref[...] + got_ref[...].astype(F32)).astype(BF16)
    shape = (META, LANES)
    live = (iota((1, LANES), 1) & (slot_rows - 1)) < count_ref[0] * tile_rows
    line = jnp.where(live, across_ref[0:1, :], -1)
    part = jnp.where(iota(shape, 0) == 0, line & 127, line >> 7)
    out_ref[n_rows:, :] = part.astype(F32).astype(BF16)


def gather_kernel(*refs, masks, slot_rows, own_lines, n_seg):
    payloads, (part_ref, send_ref, all_ref) = refs[:-3], refs[-3:]
    slab, trans = lax.axis_index("slab"), lax.axis_index("trans")
    lines = part_ref.shape[0] // 2
    depth = all_ref.shape[0]
    n_sources = len(payloads)
    block_lines = (payloads[0].shape[0] - META) // n_seg - slot_rows
    first_block = n_sources * slot_rows
    lane = iota((1, depth), 1)
    sum_line = jnp.full((1, depth), -1, jnp.int32)
    weight_line = sum_line
    if first_block + n_sources * block_lines < depth:
        used = first_block + n_sources * block_lines
        all_ref[used:, :] = jnp.zeros((depth - used, all_ref.shape[1]), F32)
    for j, ref in enumerate(payloads):
        values = ref[...].astype(F32)
        mask = jnp.where(trans == 0, masks[j][0], masks[j][1])
        taken = mask >= 0
        meta = values[n_seg * (slot_rows + block_lines) :]
        line = (meta[0:1, :] + 128.0 * meta[1:2, :]).astype(jnp.int32)
        line = jnp.concatenate([line] * (depth // LANES), axis=1)
        here = (lane >= j * slot_rows) & (lane < (j + 1) * slot_rows)
        sum_line = jnp.where(here & taken, line, sum_line)
        at = first_block + j * block_lines
        inside = lane - at
        base = (slab ^ mask) * own_lines
        weights = (inside >= 0) & (inside < own_lines) & taken
        weight_line = jnp.where(weights, base + inside, weight_line)
        measured = (inside >= own_lines) & (inside < 2 * own_lines) & taken
        sum_line = jnp.where(measured, base + inside - own_lines, sum_line)
        for a in range(n_seg):
            lanes = slice(a * LANES, (a + 1) * LANES)
            all_ref[j * slot_rows : (j + 1) * slot_rows, lanes] = values[a * slot_rows : (a + 1) * slot_rows]
            start = n_seg * slot_rows + a * block_lines
            all_ref[at : at + block_lines, lanes] = values[start : start + block_lines]
    ids = iota((lines, depth), 0)
    sign = jnp.where(lane >= first_block, -1.0, 1.0)
    chosen = jnp.concatenate(
        [jnp.where(ids == sum_line, sign, 0.0), jnp.where(ids == weight_line, 1.0, 0.0)], axis=0
    )
    part = jnp.dot(chosen.astype(BF16), all_ref[...].astype(BF16), preferred_element_type=F32)
    part_ref[...] = part
    send_ref[...] = part.astype(BF16)


def update_kernel(
    count_ref, down_ref, vol_ref, cw_ref, flat_ref, win_ref, key_ref, part_ref, got_ref,
    upd_hbm, out_hbm,
    val_ref, near_ref, upd_ref, out_ref, sems, out_sem,
    *, tile_rows,
):
    n_views, _, cols = win_ref.shape
    own_rows, shared_views, det_cols = out_ref.shape
    n_seg = det_cols // LANES
    slot_rows = key_ref.shape[0]
    slab, trans = lax.axis_index("slab"), lax.axis_index("trans")
    lines = part_ref.shape[0] // 2
    total = part_ref[...] + got_ref[...].astype(F32)
    residual = (-total[:lines] * total[lines:]).astype(BF16)
    val_ref[...] = residual.astype(F32)
    live = iota((slot_rows, 1), 0) < count_ref[0] * tile_rows
    line = jnp.where(live, down_ref[:, 0:1], -1)
    chosen = jnp.where(iota((slot_rows, lines), 1) == line, 1.0, 0.0).astype(BF16)
    near = jnp.dot(chosen, residual, preferred_element_type=F32).astype(BF16)
    for a in range(n_seg):
        at = slice(a * slot_rows, (a + 1) * slot_rows)
        near_ref[at, :LANES] = near[:, a * LANES : (a + 1) * LANES]
        if a + 1 < n_seg:
            near_ref[at, LANES:] = near[:, (a + 1) * LANES : (a + 2) * LANES]
        else:
            near_ref[at, LANES:] = jnp.zeros((slot_rows, LANES), BF16)
    n_parts = sems.shape[0]
    width = cols // n_parts
    copies = []
    for p in range(n_parts):
        at = slice(p * width, (p + 1) * width)
        key = key_ref[:, at]
        back = jnp.zeros((slot_rows, width), F32)
        for v in range(n_views):
            part = jnp.dot(near_ref[:, :WINDOW], win_ref[v, :, at], preferred_element_type=F32)
            for a in range(n_seg):
                back = jnp.where(key == v * n_seg + a, part[a * slot_rows : (a + 1) * slot_rows], back)
        gradient = lax.dot_general(
            flat_ref[...], back.astype(BF16), (((0,), (0,)), ((), ())), preferred_element_type=F32
        )
        upd_ref[:, at] = vol_ref[:, at] + 0.9 * cw_ref[:, at] * gradient
        copies.append(pltpu.make_async_copy(upd_ref.at[:, at], upd_hbm.at[:, at], sems.at[p]))
        copies[-1].start()
    for i in range(shared_views):
        for j in range(own_rows):
            line = (slab * n_views + trans * shared_views + i) * own_rows + j
            out_ref[j, i : i + 1, :] = val_ref[pl.ds(line, 1), :].astype(BF16)
    copies.append(pltpu.make_async_copy(out_ref, out_hbm, out_sem))
    copies[-1].start()
    for copy in copies:
        copy.wait()


def exchange(array, masks, n_slab):
    pairs = []
    for i in range(n_slab):
        for k, mask in enumerate(masks):
            pairs.append(((i ^ mask) * len(masks) + k, i * len(masks) + k))
    return lax.ppermute(array, ("slab", "trans"), pairs)


def direct_masks(n_group):
    half = n_group // 2
    near = list(range(1, half + 1))
    far = list(range(half + 1, n_group))
    if len(far) == 3:
        far = [far[1], far[0], far[2]]
    return list(zip(near, far + [None]))


def body(
    volume, col_weight, foot_pos, foot_width, measured, row_weight, row_tiles, tile_view_index, tile_block, tile_count
):
    n_views, cols = foot_pos.shape
    shared_views, own_rows, det_cols = measured.shape
    n_slots, tile_rows, depth = row_tiles.shape
    n_slab, n_trans = lax.axis_size("slab"), lax.axis_size("trans")
    assert n_trans == 2 and n_slab & (n_slab - 1) == 0 and n_slab > 1
    assert LANES % (n_slots * tile_rows) == 0
    n_seg = det_cols // LANES
    slot_rows = n_slots * tile_rows
    own_lines = n_views * own_rows
    lines = n_slab * own_lines
    block_lines = -(-2 * own_lines // 8) * 8
    first_rows = n_seg * (slot_rows + block_lines)
    smem, vmem = pl.BlockSpec(memory_space=pltpu.SMEM), pl.BlockSpec(memory_space=pltpu.VMEM)
    hbm = pl.BlockSpec(memory_space=pltpu.HBM)
    params = pltpu.CompilerParams(vmem_limit_bytes=32 * 1024 * 1024)
    near = (tile_view_index, tile_block, volume, foot_pos, foot_width, measured, row_weight, row_tiles)
    own, send, windows, key, flat, across, down = pl.pallas_call(
        project_kernel,
        out_shape=(
            jax.ShapeDtypeStruct((first_rows, LANES), F32),
            jax.ShapeDtypeStruct((first_rows, LANES), BF16),
            jax.ShapeDtypeStruct((n_views, WINDOW, cols), BF16),
            jax.ShapeDtypeStruct((slot_rows, cols), F32),
            jax.ShapeDtypeStruct((slot_rows, depth), BF16),
            jax.ShapeDtypeStruct((8, LANES), jnp.int32),
            jax.ShapeDtypeStruct((slot_rows, LANES), jnp.int32),
        ),
        in_specs=[hbm] * 8,
        out_specs=(vmem,) * 7,
        scratch_shapes=[
            pltpu.SMEM(tile_view_index.shape, jnp.int32),
            pltpu.SMEM(tile_block.shape, jnp.int32),
            pltpu.VMEM(volume.shape, F32),
            pltpu.VMEM(foot_pos.shape, F32),
            pltpu.VMEM(foot_width.shape, F32),
            pltpu.VMEM(measured.shape, F32),
            pltpu.VMEM(row_weight.shape, F32),
            pltpu.VMEM(row_tiles.shape, BF16),
            pltpu.VMEM((n_views, n_seg * slot_rows, cols), BF16),
            pltpu.SemaphoreType.DMA((8,)),
        ],
        compiler_params=params,
        name="project",
    )(*[pltpu.with_memory_space_constraint(array, pltpu.HBM) for array in near])

    swap = [(0, 1), (1, 0)]
    got = lax.ppermute(send, "trans", swap)
    tile_count, own = lax.optimization_barrier((tile_count, own))

    def join(*args):
        join_kernel(*args, tile_rows=tile_rows, slot_rows=slot_rows)

    payload = pl.pallas_call(
        join,
        out_shape=jax.ShapeDtypeStruct((first_rows + META, LANES), BF16),
        in_specs=[smem] + [vmem] * 3,
        out_specs=vmem,
        compiler_params=params,
        name="join",
    )(tile_count, across, own, got)

    n_group = min(GROUP, n_slab)
    steps = direct_masks(n_group)
    arrived = [exchange(payload, (a, 1 if b is None else b), n_slab) for a, b in steps]
    masks = [(-1, 0)] + [(a, -1 if b is None else b) for a, b in steps]

    def gather(*refs):
        gather_kernel(*refs, masks=masks, slot_rows=slot_rows, own_lines=own_lines, n_seg=n_seg)

    part_shape = (2 * lines, det_cols)
    all_depth = -(-len(masks) * (slot_rows + block_lines) // LANES) * LANES
    part, send = pl.pallas_call(
        gather,
        out_shape=(jax.ShapeDtypeStruct(part_shape, F32), jax.ShapeDtypeStruct(part_shape, BF16)),
        in_specs=[vmem] * len(masks),
        out_specs=(vmem,) * 2,
        scratch_shapes=[pltpu.VMEM((all_depth, det_cols), F32)],
        compiler_params=params,
        name="gather",
    )(payload, *arrived)
    bit = n_group
    while bit < n_slab:
        part = part + exchange(send, (bit, bit), n_slab).astype(F32)
        send = part.astype(BF16)
        bit *= 2
    other = lax.ppermute(send, "trans", swap)

    def update(*refs):
        update_kernel(*refs, tile_rows=tile_rows)

    n_parts = 4
    updated, residual = pl.pallas_call(
        update,
        out_shape=(
            jax.ShapeDtypeStruct(volume.shape, F32),
            jax.ShapeDtypeStruct((own_rows, shared_views, det_cols), BF16),
        ),
        in_specs=[smem] + [vmem] * 8,
        out_specs=(hbm, hbm),
        scratch_shapes=[
            pltpu.VMEM((lines, det_cols), F32),
            pltpu.VMEM((n_seg * slot_rows, 2 * LANES), BF16),
            pltpu.VMEM(volume.shape, F32),
            pltpu.VMEM((own_rows, shared_views, det_cols), BF16),
            pltpu.SemaphoreType.DMA((n_parts,)),
            pltpu.SemaphoreType.DMA(()),
        ],
        compiler_params=params,
        name="update",
    )(tile_count, down, volume, col_weight, flat, windows, key, part, other)
    return updated, jnp.transpose(residual, (1, 0, 2))


def solution(mesh):
    in_specs = (
        P(("groups", "slab"), "trans"),
        P(("groups", "slab"), "trans"),
        P(None, "trans"),
        P(None, "trans"),
        P(("groups", "trans"), "slab", None),
        P(("groups", "trans"), "slab", None),
        P(("groups", "slab"), None, None),
        P(("groups", "slab")),
        P(("groups", "slab")),
        P(("groups", "slab")),
    )
    out_specs = (P(("groups", "slab"), "trans"), P(("groups", "trans"), "slab", None))
    return jax.shard_map(body, mesh=mesh, in_specs=in_specs, out_specs=out_specs, check_vma=False)
```

```python
import jax
import jax.numpy as jnp
from jax import lax
from jax.experimental import pallas as pl
from jax.experimental.pallas import tpu as pltpu
from jax.sharding import PartitionSpec as P

LANES = 128
WINDOW = 144
GROUP = 8
META = 16
F32 = jnp.float32
BF16 = jnp.bfloat16


def iota(shape, dim):
    return lax.broadcasted_iota(jnp.int32, shape, dim)


def segment_of(pos, width, n_seg):
    first = jnp.floor((pos - width - 0.5) * (1.0 / LANES))
    return jnp.clip(first, 0.0, n_seg - 1.0)


def slot_vector(values, repeat, index):
    result = jnp.full(index.shape, values[0], jnp.int32)
    for s in range(1, len(values)):
        result = jnp.where(index >= s * repeat, values[s], result)
    return result


def slot_lines(view_ref, block_ref, tile_rows, n_views, own_rows):
    lines = []
    for s in range(view_ref.shape[0]):
        for r in range(tile_rows):
            detector_row = block_ref[s] * tile_rows + r
            lines.append((detector_row // own_rows * n_views + view_ref[s]) * own_rows + detector_row % own_rows)
    return lines


def project_kernel(
    view_hbm, block_hbm, vol_hbm, pos_hbm, wid_hbm, meas_hbm, rw_hbm, tiles_hbm,
    own_ref, send_ref, win_ref, key_ref, flat_ref, across_ref, down_ref,
    view_ref, block_ref, vol_ref, pos_ref, wid_ref, meas_ref, rw_ref, tiles_ref, spread_ref, sems,
):
    inputs = (pos_hbm, wid_hbm, vol_hbm, view_hbm, block_hbm, tiles_hbm, meas_hbm, rw_hbm)
    holders = (pos_ref, wid_ref, vol_ref, view_ref, block_ref, tiles_ref, meas_ref, rw_ref)
    copies = [pltpu.make_async_copy(a, b, sems.at[i]) for i, (a, b) in enumerate(zip(inputs, holders))]
    for copy in copies:
        copy.start()
    n_views, cols = pos_ref.shape
    n_slots, tile_rows, _ = tiles_ref.shape
    shared_views, own_rows, det_cols = meas_ref.shape
    n_seg = det_cols // LANES
    slot_rows = n_slots * tile_rows
    own_lines = n_views * own_rows
    trans = lax.axis_index("trans")
    offsets = iota((WINDOW, cols), 0).astype(F32)
    copies[0].wait()
    copies[1].wait()
    segments = []
    for v in range(n_views):
        segments.append(segment_of(pos_ref[v : v + 1, :], wid_ref[v : v + 1, :], n_seg))

    def window(v):
        pos, wid = pos_ref[v : v + 1, :], wid_ref[v : v + 1, :]
        distance = jnp.abs(offsets + (segments[v] * LANES + 0.5 - pos)) * (1.0 / wid)
        win_ref[v] = jnp.maximum(0.0, 1.0 - distance).astype(BF16)

    first_views = n_views // 2
    for v in range(first_views):
        window(v)
    for copy in copies[2:]:
        copy.wait()
    tiles = tiles_ref[...].astype(F32)
    flat = jnp.concatenate([tiles[s, r : r + 1, :] for s in range(n_slots) for r in range(tile_rows)], axis=0)
    flat = flat.astype(BF16)
    flat_ref[...] = flat
    rows = jnp.dot(flat, vol_ref[...].astype(BF16), preferred_element_type=F32)
    views = slot_vector([view_ref[s] for s in range(n_slots)], tile_rows, iota((slot_rows, cols), 0))
    key = jnp.broadcast_to(segments[0], (slot_rows, cols))
    for v in range(1, n_views):
        key = jnp.where(views == v, segments[v] + float(v * n_seg), key)
    key_ref[...] = key
    sums = jnp.zeros((n_seg * slot_rows, WINDOW), F32)
    for v in range(n_views):
        for a in range(n_seg):
            spread_ref[v, a * slot_rows : (a + 1) * slot_rows, :] = jnp.where(key == v * n_seg + a, rows, 0.0).astype(BF16)
        if v >= first_views:
            window(v)
        sums = sums + lax.dot_general(
            spread_ref[v], win_ref[v], (((1,), (1,)), ((), ())), preferred_element_type=F32
        )
    numbers = slot_lines(view_ref, block_ref, tile_rows, n_views, own_rows)
    across_ref[...] = slot_vector(numbers, 1, iota(across_ref.shape, 1) & (slot_rows - 1))
    down_ref[...] = slot_vector(numbers, 1, iota(down_ref.shape, 0))
    lines = own_ref.shape[0] // n_seg - slot_rows
    place = iota((lines, det_cols), 0)
    block = jnp.zeros((lines, det_cols), F32)
    for i in range(shared_views):
        for j in range(own_rows):
            at = (trans * shared_views + i) * own_rows + j
            block = jnp.where(place == at, rw_ref[i, j : j + 1, :], block)
            block = jnp.where(place == own_lines + at, meas_ref[i, j : j + 1, :], block)
    for a in range(n_seg):
        at = n_seg * slot_rows + a * lines
        own_ref[at : at + lines, :] = block[:, a * LANES : (a + 1) * LANES]
    edge = WINDOW - LANES
    own_ref[: n_seg * slot_rows, :] = sums[:, :LANES]
    own_ref[slot_rows : n_seg * slot_rows, :edge] += sums[: (n_seg - 1) * slot_rows, LANES:]
    send_ref[...] = own_ref[...].astype(BF16)


def join_kernel(count_ref, across_ref, down_ref, own_ref, got_ref, out_ref, wanted_ref, *, tile_rows, own_lines):
    n_rows = own_ref.shape[0]
    slot_rows = down_ref.shape[0]
    out_ref[:n_rows, :] = (own_ref[...] + got_ref[...].astype(F32)).astype(BF16)
    shape = (META, LANES)
    live_rows = count_ref[0] * tile_rows
    live = (iota((1, LANES), 1) & (slot_rows - 1)) < live_rows
    line = jnp.where(live, across_ref[0:1, :], -1)
    part = jnp.where(iota(shape, 0) == 0, line & 127, line >> 7)
    out_ref[n_rows:, :] = part.astype(F32).astype(BF16)
    wanted_ref[:slot_rows, :] = jnp.where(iota((slot_rows, LANES), 0) < live_rows, down_ref[...], -2)
    shape = (wanted_ref.shape[0] - slot_rows, LANES)
    index = iota(shape, 0)
    wanted_ref[slot_rows:, :] = jnp.where(index < own_lines, lax.axis_index("slab") * own_lines + index, -2)


def gather_kernel(ids_ref, *refs, masks, slot_rows, own_lines, n_seg):
    payloads, (part_ref, send_ref, all_ref) = refs[:-3], refs[-3:]
    slab, trans = lax.axis_index("slab"), lax.axis_index("trans")
    depth = all_ref.shape[0]
    n_sources = len(payloads)
    block_lines = (payloads[0].shape[0] - META) // n_seg - slot_rows
    first_block = n_sources * slot_rows
    lane = iota((1, depth), 1)
    sum_line = jnp.full((1, depth), -1, jnp.int32)
    weight_line = sum_line
    if first_block + n_sources * block_lines < depth:
        used = first_block + n_sources * block_lines
        all_ref[used:, :] = jnp.zeros((depth - used, all_ref.shape[1]), F32)
    for j, ref in enumerate(payloads):
        values = ref[...].astype(F32)
        mask = jnp.where(trans == 0, masks[j][0], masks[j][1])
        taken = mask >= 0
        meta = values[n_seg * (slot_rows + block_lines) :]
        line = (meta[0:1, :] + 128.0 * meta[1:2, :]).astype(jnp.int32)
        line = jnp.concatenate([line] * (depth // LANES), axis=1)
        here = (lane >= j * slot_rows) & (lane < (j + 1) * slot_rows)
        sum_line = jnp.where(here & taken, line, sum_line)
        at = first_block + j * block_lines
        inside = lane - at
        base = (slab ^ mask) * own_lines
        weights = (inside >= 0) & (inside < own_lines) & taken
        weight_line = jnp.where(weights, base + inside, weight_line)
        measured = (inside >= own_lines) & (inside < 2 * own_lines) & taken
        sum_line = jnp.where(measured, base + inside - own_lines, sum_line)
        for a in range(n_seg):
            lanes = slice(a * LANES, (a + 1) * LANES)
            all_ref[j * slot_rows : (j + 1) * slot_rows, lanes] = values[a * slot_rows : (a + 1) * slot_rows]
            start = n_seg * slot_rows + a * block_lines
            all_ref[at : at + block_lines, lanes] = values[start : start + block_lines]
    ids = jnp.concatenate([ids_ref[...]] * (depth // LANES), axis=1)
    sign = jnp.where(lane >= first_block, -1.0, 1.0)
    chosen = jnp.concatenate(
        [jnp.where(ids == sum_line, sign, 0.0), jnp.where(ids == weight_line, 1.0, 0.0)], axis=0
    )
    part = jnp.dot(chosen.astype(BF16), all_ref[...].astype(BF16), preferred_element_type=F32)
    part_ref[...] = part
    send_ref[...] = part.astype(BF16)


def pick_kernel(ids_ref, part_ref, out_ref, send_ref):
    lines = part_ref.shape[0] // 2
    ids = jnp.concatenate([ids_ref[...]] * (-(-lines // LANES)), axis=1)[:, :lines]
    chosen = (iota(ids.shape, 1) == ids).astype(F32)
    for half in range(2):
        part = part_ref[half * lines : (half + 1) * lines, :]
        rows = slice(half * ids.shape[0], (half + 1) * ids.shape[0])
        picked = jnp.dot(chosen, part, preferred_element_type=F32, precision=lax.Precision.HIGHEST)
        out_ref[rows, :] = picked
        send_ref[rows, :] = picked.astype(BF16)


def update_kernel(
    vol_ref, cw_ref, flat_ref, win_ref, key_ref, part_ref, got_ref,
    upd_hbm, out_hbm,
    val_ref, near_ref, upd_ref, out_ref, sems, out_sem,
):
    n_views, _, cols = win_ref.shape
    own_rows, shared_views, det_cols = out_ref.shape
    n_seg = det_cols // LANES
    slot_rows = key_ref.shape[0]
    trans = lax.axis_index("trans")
    lines = part_ref.shape[0] // 2
    total = part_ref[...] + got_ref[...].astype(F32)
    residual = -total[:lines] * total[lines:]
    near = residual[:slot_rows].astype(BF16)
    val_ref[...] = residual[slot_rows:]
    for a in range(n_seg):
        at = slice(a * slot_rows, (a + 1) * slot_rows)
        near_ref[at, :LANES] = near[:, a * LANES : (a + 1) * LANES]
        if a + 1 < n_seg:
            near_ref[at, LANES:] = near[:, (a + 1) * LANES : (a + 2) * LANES]
        else:
            near_ref[at, LANES:] = jnp.zeros((slot_rows, LANES), BF16)
    for i in range(shared_views):
        for j in range(own_rows):
            line = (trans * shared_views + i) * own_rows + j
            out_ref[j, i : i + 1, :] = val_ref[pl.ds(line, 1), :].astype(BF16)
    copies = [pltpu.make_async_copy(out_ref, out_hbm, out_sem)]
    copies[0].start()
    key = key_ref[...]
    back = jnp.zeros((slot_rows, cols), F32)
    for v in range(n_views):
        part = jnp.dot(near_ref[:, :WINDOW], win_ref[v], preferred_element_type=F32)
        for a in range(n_seg):
            back = jnp.where(key == v * n_seg + a, part[a * slot_rows : (a + 1) * slot_rows], back)
    gradient = lax.dot_general(flat_ref[...], back.astype(BF16), (((0,), (0,)), ((), ())), preferred_element_type=F32)
    n_parts = sems.shape[0]
    depth = gradient.shape[0] // n_parts
    for p in range(n_parts):
        at = slice(p * depth, (p + 1) * depth)
        upd_ref[at, :] = vol_ref[at, :] + cw_ref[at, :] * gradient[at]
        copies.append(pltpu.make_async_copy(upd_ref.at[at, :], upd_hbm.at[at, :], sems.at[p]))
        copies[-1].start()
    for copy in copies:
        copy.wait()


def exchange(array, masks, n_slab):
    pairs = []
    for i in range(n_slab):
        for k, mask in enumerate(masks):
            pairs.append(((i ^ mask) * len(masks) + k, i * len(masks) + k))
    return lax.ppermute(array, ("slab", "trans"), pairs)


def direct_steps(n_group):
    half = n_group // 2
    near = [(mask, True) for mask in range(half, 0, -1)]
    far = [(1, False)] + [(mask, True) for mask in range(n_group - 1, half, -1)]
    if n_group == 8:
        near = [(mask, True) for mask in (4, 1, 2, 3)]
        far = [(1, False), (7, True), (5, True), (6, True)]
    return list(zip(near, far))


def body(
    volume, col_weight, foot_pos, foot_width, measured, row_weight, row_tiles, tile_view_index, tile_block, tile_count
):
    n_views, cols = foot_pos.shape
    shared_views, own_rows, det_cols = measured.shape
    n_slots, tile_rows, depth = row_tiles.shape
    n_slab, n_trans = lax.axis_size("slab"), lax.axis_size("trans")
    assert n_trans == 2 and n_slab & (n_slab - 1) == 0 and n_slab > 1
    assert LANES % (n_slots * tile_rows) == 0
    n_seg = det_cols // LANES
    slot_rows = n_slots * tile_rows
    own_lines = n_views * own_rows
    lines = n_slab * own_lines
    block_lines = -(-2 * own_lines // 8) * 8
    first_rows = n_seg * (slot_rows + block_lines)
    smem, vmem = pl.BlockSpec(memory_space=pltpu.SMEM), pl.BlockSpec(memory_space=pltpu.VMEM)
    hbm = pl.BlockSpec(memory_space=pltpu.HBM)
    params = pltpu.CompilerParams(vmem_limit_bytes=32 * 1024 * 1024)
    near = (tile_view_index, tile_block, volume, foot_pos, foot_width, measured, row_weight, row_tiles)
    own, send, windows, key, flat, across, down = pl.pallas_call(
        project_kernel,
        out_shape=(
            jax.ShapeDtypeStruct((first_rows, LANES), F32),
            jax.ShapeDtypeStruct((first_rows, LANES), BF16),
            jax.ShapeDtypeStruct((n_views, WINDOW, cols), BF16),
            jax.ShapeDtypeStruct((slot_rows, cols), F32),
            jax.ShapeDtypeStruct((slot_rows, depth), BF16),
            jax.ShapeDtypeStruct((8, LANES), jnp.int32),
            jax.ShapeDtypeStruct((slot_rows, LANES), jnp.int32),
        ),
        in_specs=[hbm] * 8,
        out_specs=(vmem,) * 7,
        scratch_shapes=[
            pltpu.SMEM(tile_view_index.shape, jnp.int32),
            pltpu.SMEM(tile_block.shape, jnp.int32),
            pltpu.VMEM(volume.shape, F32),
            pltpu.VMEM(foot_pos.shape, F32),
            pltpu.VMEM(foot_width.shape, F32),
            pltpu.VMEM(measured.shape, F32),
            pltpu.VMEM(row_weight.shape, F32),
            pltpu.VMEM(row_tiles.shape, BF16),
            pltpu.VMEM((n_views, n_seg * slot_rows, cols), BF16),
            pltpu.SemaphoreType.DMA((8,)),
        ],
        compiler_params=params,
        name="project",
    )(*[pltpu.with_memory_space_constraint(array, pltpu.HBM) for array in near])

    swap = [(0, 1), (1, 0)]
    got = lax.ppermute(send, "trans", swap)
    tile_count, own = lax.optimization_barrier((tile_count, own))

    def join(*refs):
        join_kernel(*refs, tile_rows=tile_rows, own_lines=own_lines)

    n_wanted = slot_rows + -(-own_lines // 8) * 8
    payload, wanted = pl.pallas_call(
        join,
        out_shape=(
            jax.ShapeDtypeStruct((first_rows + META, LANES), BF16),
            jax.ShapeDtypeStruct((n_wanted, LANES), jnp.int32),
        ),
        in_specs=[smem] + [vmem] * 4,
        out_specs=(vmem,) * 2,
        compiler_params=params,
        name="join",
    )(tile_count, across, down, own, got)

    n_group = min(GROUP, n_slab)
    steps = direct_steps(n_group)
    arrived = [exchange(payload, [mask for mask, _ in step], n_slab) for step in steps]
    masks = [[mask if used else -1 for mask, used in step] for step in steps]

    def gather(*refs):
        gather_kernel(*refs, masks=[(-1, 0)] + masks, slot_rows=slot_rows, own_lines=own_lines, n_seg=n_seg)

    whole = n_group == n_slab
    ids = wanted if whole else jnp.broadcast_to(jnp.arange(lines, dtype=jnp.int32)[:, None], (lines, LANES))
    part_shape = (2 * ids.shape[0], det_cols)
    all_depth = -(-(1 + len(steps)) * (slot_rows + block_lines) // LANES) * LANES
    part, send = pl.pallas_call(
        gather,
        out_shape=(jax.ShapeDtypeStruct(part_shape, F32), jax.ShapeDtypeStruct(part_shape, BF16)),
        in_specs=[vmem] * (2 + len(steps)),
        out_specs=(vmem,) * 2,
        scratch_shapes=[pltpu.VMEM((all_depth, det_cols), F32)],
        compiler_params=params,
        name="gather",
    )(ids, payload, *arrived)
    if not whole:
        bit = n_group
        while bit < n_slab:
            part = part + exchange(part.astype(BF16), (bit, bit), n_slab).astype(F32)
            bit *= 2
        part_shape = (2 * n_wanted, det_cols)
        part, send = pl.pallas_call(
            pick_kernel,
            out_shape=(jax.ShapeDtypeStruct(part_shape, F32), jax.ShapeDtypeStruct(part_shape, BF16)),
            in_specs=[vmem] * 2,
            out_specs=(vmem,) * 2,
            compiler_params=params,
            name="pick",
        )(wanted, part)
    scaled, send = lax.optimization_barrier((0.9 * col_weight, send))
    other = lax.ppermute(send, "trans", swap)

    n_parts = 2
    updated, residual = pl.pallas_call(
        update_kernel,
        out_shape=(
            jax.ShapeDtypeStruct(volume.shape, F32),
            jax.ShapeDtypeStruct((own_rows, shared_views, det_cols), BF16),
        ),
        in_specs=[vmem] * 7,
        out_specs=(hbm, hbm),
        scratch_shapes=[
            pltpu.VMEM((n_wanted - slot_rows, det_cols), F32),
            pltpu.VMEM((n_seg * slot_rows, 2 * LANES), BF16),
            pltpu.VMEM(volume.shape, F32),
            pltpu.VMEM((own_rows, shared_views, det_cols), BF16),
            pltpu.SemaphoreType.DMA((n_parts,)),
            pltpu.SemaphoreType.DMA(()),
        ],
        compiler_params=params,
        name="update",
    )(volume, scaled, flat, windows, key, part, other)
    return updated, jnp.transpose(residual, (1, 0, 2))


def solution(mesh):
    in_specs = (
        P(("groups", "slab"), "trans"),
        P(("groups", "slab"), "trans"),
        P(None, "trans"),
        P(None, "trans"),
        P(("groups", "trans"), "slab", None),
        P(("groups", "trans"), "slab", None),
        P(("groups", "slab"), None, None),
        P(("groups", "slab")),
        P(("groups", "slab")),
        P(("groups", "slab")),
    )
    out_specs = (P(("groups", "slab"), "trans"), P(("groups", "trans"), "slab", None))
    return jax.shard_map(body, mesh=mesh, in_specs=in_specs, out_specs=out_specs, check_vma=False)
```

```python
import jax
import jax.numpy as jnp
from jax import lax
from jax.experimental import pallas as pl
from jax.experimental.pallas import tpu as pltpu
from jax.sharding import PartitionSpec as P

LANES = 128
WINDOW = 144
GROUP = 8
META = 8
F32 = jnp.float32
BF16 = jnp.bfloat16


def iota(shape, dim):
    return lax.broadcasted_iota(jnp.int32, shape, dim)


def segment_of(pos, width, n_seg):
    first = jnp.floor((pos - width - 0.5) * (1.0 / LANES))
    return jnp.clip(first, 0.0, n_seg - 1.0)


def slot_vector(values, repeat, index):
    result = jnp.full(index.shape, values[0], jnp.int32)
    for s in range(1, len(values)):
        result = jnp.where(index >= s * repeat, values[s], result)
    return result


def slot_lines(view_ref, block_ref, tile_rows, n_views, own_rows):
    lines = []
    for s in range(view_ref.shape[0]):
        for r in range(tile_rows):
            detector_row = block_ref[s] * tile_rows + r
            lines.append((detector_row // own_rows * n_views + view_ref[s]) * own_rows + detector_row % own_rows)
    return lines


def project_kernel(
    view_hbm, block_hbm, vol_hbm, pos_hbm, wid_hbm, meas_hbm, rw_hbm, tiles_hbm,
    own_ref, send_ref, win_ref, key_ref, flat_ref, across_ref, down_ref,
    view_ref, block_ref, vol_ref, pos_ref, wid_ref, meas_ref, rw_ref, tiles_ref, spread_ref, sems,
):
    inputs = (pos_hbm, wid_hbm, vol_hbm, view_hbm, block_hbm, tiles_hbm, meas_hbm, rw_hbm)
    holders = (pos_ref, wid_ref, vol_ref, view_ref, block_ref, tiles_ref, meas_ref, rw_ref)
    copies = [pltpu.make_async_copy(a, b, sems.at[i]) for i, (a, b) in enumerate(zip(inputs, holders))]
    for copy in copies:
        copy.start()
    n_views, cols = pos_ref.shape
    n_slots, tile_rows, _ = tiles_ref.shape
    shared_views, own_rows, det_cols = meas_ref.shape
    n_seg = det_cols // LANES
    slot_rows = n_slots * tile_rows
    own_lines = n_views * own_rows
    trans = lax.axis_index("trans")
    offsets = iota((WINDOW, cols), 0).astype(F32)
    copies[0].wait()
    copies[1].wait()
    segments = []
    for v in range(n_views):
        segments.append(segment_of(pos_ref[v : v + 1, :], wid_ref[v : v + 1, :], n_seg))

    def window(v):
        pos, wid = pos_ref[v : v + 1, :], wid_ref[v : v + 1, :]
        distance = jnp.abs(offsets + (segments[v] * LANES + 0.5 - pos)) * (1.0 / wid)
        win_ref[v] = jnp.maximum(0.0, 1.0 - distance).astype(BF16)

    first_views = n_views // 2
    for v in range(first_views):
        window(v)
    for copy in copies[2:]:
        copy.wait()
    tiles = tiles_ref[...].astype(F32)
    flat = jnp.concatenate([tiles[s, r : r + 1, :] for s in range(n_slots) for r in range(tile_rows)], axis=0)
    flat = flat.astype(BF16)
    flat_ref[...] = flat
    rows = jnp.dot(flat, vol_ref[...].astype(BF16), preferred_element_type=F32)
    views = slot_vector([view_ref[s] for s in range(n_slots)], tile_rows, iota((slot_rows, cols), 0))
    key = jnp.broadcast_to(segments[0], (slot_rows, cols))
    for v in range(1, n_views):
        key = jnp.where(views == v, segments[v] + float(v * n_seg), key)
    key_ref[...] = key
    sums = jnp.zeros((n_seg * slot_rows, WINDOW), F32)
    for v in range(n_views):
        for a in range(n_seg):
            spread_ref[v, a * slot_rows : (a + 1) * slot_rows, :] = jnp.where(key == v * n_seg + a, rows, 0.0).astype(BF16)
        if v >= first_views:
            window(v)
        sums = sums + lax.dot_general(
            spread_ref[v], win_ref[v], (((1,), (1,)), ((), ())), preferred_element_type=F32
        )
    numbers = slot_lines(view_ref, block_ref, tile_rows, n_views, own_rows)
    across_ref[...] = slot_vector(numbers, 1, iota(across_ref.shape, 1) & (slot_rows - 1))
    down_ref[...] = slot_vector(numbers, 1, iota(down_ref.shape, 0))
    lines = own_ref.shape[0] // n_seg - slot_rows
    place = iota((lines, det_cols), 0)
    block = jnp.zeros((lines, det_cols), F32)
    for i in range(shared_views):
        for j in range(own_rows):
            at = (trans * shared_views + i) * own_rows + j
            block = jnp.where(place == at, rw_ref[i, j : j + 1, :], block)
            block = jnp.where(place == own_lines + at, meas_ref[i, j : j + 1, :], block)
    for a in range(n_seg):
        at = n_seg * slot_rows + a * lines
        own_ref[at : at + lines, :] = block[:, a * LANES : (a + 1) * LANES]
    edge = WINDOW - LANES
    own_ref[: n_seg * slot_rows, :] = sums[:, :LANES]
    own_ref[slot_rows : n_seg * slot_rows, :edge] += sums[: (n_seg - 1) * slot_rows, LANES:]
    send_ref[...] = own_ref[...].astype(BF16)


def join_kernel(count_ref, across_ref, down_ref, own_ref, got_ref, out_ref, wanted_ref, *, tile_rows, own_lines):
    n_rows = own_ref.shape[0]
    slot_rows = down_ref.shape[0]
    out_ref[:n_rows, :] = (own_ref[...] + got_ref[...].astype(F32)).astype(BF16)
    shape = (META, LANES)
    live_rows = count_ref[0] * tile_rows
    live = (iota((1, LANES), 1) & (slot_rows - 1)) < live_rows
    line = jnp.where(live, across_ref[0:1, :], -1)
    part = jnp.where(iota(shape, 0) == 0, line & 127, line >> 7)
    out_ref[n_rows:, :] = part.astype(F32).astype(BF16)
    wanted_ref[:slot_rows, :] = jnp.where(iota((slot_rows, LANES), 0) < live_rows, down_ref[...], -2)
    shape = (wanted_ref.shape[0] - slot_rows, LANES)
    index = iota(shape, 0)
    wanted_ref[slot_rows:, :] = jnp.where(index < own_lines, lax.axis_index("slab") * own_lines + index, -2)


def gather_kernel(ids_ref, *refs, masks, slot_rows, own_lines, n_seg):
    payloads, (part_ref, send_ref, all_ref) = refs[:-3], refs[-3:]
    slab, trans = lax.axis_index("slab"), lax.axis_index("trans")
    depth = all_ref.shape[0]
    n_sources = len(payloads)
    block_lines = (payloads[0].shape[0] - META) // n_seg - slot_rows
    first_block = n_sources * slot_rows
    lane = iota((1, depth), 1)
    sum_line = jnp.full((1, depth), -1, jnp.int32)
    weight_line = sum_line
    if first_block + n_sources * block_lines < depth:
        used = first_block + n_sources * block_lines
        all_ref[used:, :] = jnp.zeros((depth - used, all_ref.shape[1]), F32)
    for j, ref in enumerate(payloads):
        values = ref[...].astype(F32)
        mask = jnp.where(trans == 0, masks[j][0], masks[j][1])
        taken = mask >= 0
        meta = values[n_seg * (slot_rows + block_lines) :]
        line = (meta[0:1, :] + 128.0 * meta[1:2, :]).astype(jnp.int32)
        line = jnp.concatenate([line] * (depth // LANES), axis=1)
        here = (lane >= j * slot_rows) & (lane < (j + 1) * slot_rows)
        sum_line = jnp.where(here & taken, line, sum_line)
        at = first_block + j * block_lines
        inside = lane - at
        base = (slab ^ mask) * own_lines
        weights = (inside >= 0) & (inside < own_lines) & taken
        weight_line = jnp.where(weights, base + inside, weight_line)
        measured = (inside >= own_lines) & (inside < 2 * own_lines) & taken
        sum_line = jnp.where(measured, base + inside - own_lines, sum_line)
        for a in range(n_seg):
            lanes = slice(a * LANES, (a + 1) * LANES)
            all_ref[j * slot_rows : (j + 1) * slot_rows, lanes] = values[a * slot_rows : (a + 1) * slot_rows]
            start = n_seg * slot_rows + a * block_lines
            all_ref[at : at + block_lines, lanes] = values[start : start + block_lines]
    ids = jnp.concatenate([ids_ref[...]] * (depth // LANES), axis=1)
    sign = jnp.where(lane >= first_block, -1.0, 1.0)
    chosen = jnp.concatenate(
        [jnp.where(ids == sum_line, sign, 0.0), jnp.where(ids == weight_line, 1.0, 0.0)], axis=0
    )
    part = jnp.dot(chosen.astype(BF16), all_ref[...].astype(BF16), preferred_element_type=F32)
    part_ref[...] = part
    send_ref[...] = part.astype(BF16)


def pick_kernel(ids_ref, part_ref, out_ref, send_ref):
    lines = part_ref.shape[0] // 2
    ids = jnp.concatenate([ids_ref[...]] * (-(-lines // LANES)), axis=1)[:, :lines]
    chosen = (iota(ids.shape, 1) == ids).astype(F32)
    for half in range(2):
        part = part_ref[half * lines : (half + 1) * lines, :]
        rows = slice(half * ids.shape[0], (half + 1) * ids.shape[0])
        picked = jnp.dot(chosen, part, preferred_element_type=F32, precision=lax.Precision.HIGHEST)
        out_ref[rows, :] = picked
        send_ref[rows, :] = picked.astype(BF16)


def update_kernel(
    vol_ref, cw_ref, flat_ref, win_ref, key_ref, part_ref, got_ref,
    upd_hbm, out_hbm,
    val_ref, near_ref, upd_ref, out_ref, sems, out_sem,
):
    n_views, _, cols = win_ref.shape
    own_rows, shared_views, det_cols = out_ref.shape
    n_seg = det_cols // LANES
    slot_rows = key_ref.shape[0]
    trans = lax.axis_index("trans")
    lines = part_ref.shape[0] // 2
    total = part_ref[...] + got_ref[...].astype(F32)
    residual = -total[:lines] * total[lines:]
    near = residual[:slot_rows].astype(BF16)
    val_ref[...] = residual[slot_rows:]
    for a in range(n_seg):
        at = slice(a * slot_rows, (a + 1) * slot_rows)
        near_ref[at, :LANES] = near[:, a * LANES : (a + 1) * LANES]
        if a + 1 < n_seg:
            near_ref[at, LANES:] = near[:, (a + 1) * LANES : (a + 2) * LANES]
        else:
            near_ref[at, LANES:] = jnp.zeros((slot_rows, LANES), BF16)
    for i in range(shared_views):
        for j in range(own_rows):
            line = (trans * shared_views + i) * own_rows + j
            out_ref[j, i : i + 1, :] = val_ref[pl.ds(line, 1), :].astype(BF16)
    copies = [pltpu.make_async_copy(out_ref, out_hbm, out_sem)]
    copies[0].start()
    n_parts = sems.shape[0]
    width = cols // n_parts
    spans = [slice(p * width, (p + 1) * width) for p in range(n_parts)]
    near_all = near_ref[:, :WINDOW]
    parts = [[jnp.dot(near_all, win_ref[v, :, at], preferred_element_type=F32) for v in range(n_views)] for at in spans]
    gradients = []
    for p, at in enumerate(spans):
        key = key_ref[:, at]
        back = jnp.zeros((slot_rows, width), F32)
        for v in range(n_views):
            for a in range(n_seg):
                back = jnp.where(key == v * n_seg + a, parts[p][v][a * slot_rows : (a + 1) * slot_rows], back)
        gradient = lax.dot_general(
            flat_ref[...], back.astype(BF16), (((0,), (0,)), ((), ())), preferred_element_type=F32
        )
        upd_ref[:, at] = vol_ref[:, at] + cw_ref[:, at] * gradient
        copies.append(pltpu.make_async_copy(upd_ref.at[:, at], upd_hbm.at[:, at], sems.at[p]))
        copies[-1].start()
    for copy in copies:
        copy.wait()


def exchange(array, masks, n_slab):
    pairs = []
    for i in range(n_slab):
        for k, mask in enumerate(masks):
            pairs.append(((i ^ mask) * len(masks) + k, i * len(masks) + k))
    return lax.ppermute(array, ("slab", "trans"), pairs)


def direct_steps(n_group):
    half = n_group // 2
    near = [(mask, True) for mask in range(half, 0, -1)]
    far = [(1, False)] + [(mask, True) for mask in range(n_group - 1, half, -1)]
    if n_group == 8:
        near = [(mask, True) for mask in (4, 1, 3, 2)]
        far = [(1, False), (7, True), (5, True), (6, True)]
    return list(zip(near, far))


def body(
    volume, col_weight, foot_pos, foot_width, measured, row_weight, row_tiles, tile_view_index, tile_block, tile_count
):
    n_views, cols = foot_pos.shape
    shared_views, own_rows, det_cols = measured.shape
    n_slots, tile_rows, depth = row_tiles.shape
    n_slab, n_trans = lax.axis_size("slab"), lax.axis_size("trans")
    assert n_trans == 2 and n_slab & (n_slab - 1) == 0 and n_slab > 1
    assert LANES % (n_slots * tile_rows) == 0
    n_seg = det_cols // LANES
    slot_rows = n_slots * tile_rows
    own_lines = n_views * own_rows
    lines = n_slab * own_lines
    block_lines = -(-2 * own_lines // 8) * 8
    first_rows = n_seg * (slot_rows + block_lines)
    smem, vmem = pl.BlockSpec(memory_space=pltpu.SMEM), pl.BlockSpec(memory_space=pltpu.VMEM)
    hbm = pl.BlockSpec(memory_space=pltpu.HBM)
    params = pltpu.CompilerParams(vmem_limit_bytes=32 * 1024 * 1024)
    near = (tile_view_index, tile_block, volume, foot_pos, foot_width, measured, row_weight, row_tiles)
    own, send, windows, key, flat, across, down = pl.pallas_call(
        project_kernel,
        out_shape=(
            jax.ShapeDtypeStruct((first_rows, LANES), F32),
            jax.ShapeDtypeStruct((first_rows, LANES), BF16),
            jax.ShapeDtypeStruct((n_views, WINDOW, cols), BF16),
            jax.ShapeDtypeStruct((slot_rows, cols), F32),
            jax.ShapeDtypeStruct((slot_rows, depth), BF16),
            jax.ShapeDtypeStruct((8, LANES), jnp.int32),
            jax.ShapeDtypeStruct((slot_rows, LANES), jnp.int32),
        ),
        in_specs=[hbm] * 8,
        out_specs=(vmem,) * 7,
        scratch_shapes=[
            pltpu.SMEM(tile_view_index.shape, jnp.int32),
            pltpu.SMEM(tile_block.shape, jnp.int32),
            pltpu.VMEM(volume.shape, F32),
            pltpu.VMEM(foot_pos.shape, F32),
            pltpu.VMEM(foot_width.shape, F32),
            pltpu.VMEM(measured.shape, F32),
            pltpu.VMEM(row_weight.shape, F32),
            pltpu.VMEM(row_tiles.shape, BF16),
            pltpu.VMEM((n_views, n_seg * slot_rows, cols), BF16),
            pltpu.SemaphoreType.DMA((8,)),
        ],
        compiler_params=params,
        name="project",
    )(*[pltpu.with_memory_space_constraint(array, pltpu.HBM) for array in near])

    swap = [(0, 1), (1, 0)]
    got = lax.ppermute(send, "trans", swap)
    tile_count, own = lax.optimization_barrier((tile_count, own))

    def join(*refs):
        join_kernel(*refs, tile_rows=tile_rows, own_lines=own_lines)

    n_wanted = slot_rows + -(-own_lines // 8) * 8
    payload, wanted = pl.pallas_call(
        join,
        out_shape=(
            jax.ShapeDtypeStruct((first_rows + META, LANES), BF16),
            jax.ShapeDtypeStruct((n_wanted, LANES), jnp.int32),
        ),
        in_specs=[smem] + [vmem] * 4,
        out_specs=(vmem,) * 2,
        compiler_params=params,
        name="join",
    )(tile_count, across, down, own, got)

    n_group = min(GROUP, n_slab)
    steps = direct_steps(n_group)
    arrived = [exchange(payload, [mask for mask, _ in step], n_slab) for step in steps]
    masks = [[mask if used else -1 for mask, used in step] for step in steps]

    def gather(*refs):
        gather_kernel(*refs, masks=[(-1, 0)] + masks, slot_rows=slot_rows, own_lines=own_lines, n_seg=n_seg)

    whole = n_group == n_slab
    ids = wanted if whole else jnp.broadcast_to(jnp.arange(lines, dtype=jnp.int32)[:, None], (lines, LANES))
    part_shape = (2 * ids.shape[0], det_cols)
    all_depth = -(-(1 + len(steps)) * (slot_rows + block_lines) // LANES) * LANES
    part, send = pl.pallas_call(
        gather,
        out_shape=(jax.ShapeDtypeStruct(part_shape, F32), jax.ShapeDtypeStruct(part_shape, BF16)),
        in_specs=[vmem] * (2 + len(steps)),
        out_specs=(vmem,) * 2,
        scratch_shapes=[pltpu.VMEM((all_depth, det_cols), F32)],
        compiler_params=params,
        name="gather",
    )(ids, payload, *arrived)
    if not whole:
        bit = n_group
        while bit < n_slab:
            part = part + exchange(part.astype(BF16), (bit, bit), n_slab).astype(F32)
            bit *= 2
        part_shape = (2 * n_wanted, det_cols)
        part, send = pl.pallas_call(
            pick_kernel,
            out_shape=(jax.ShapeDtypeStruct(part_shape, F32), jax.ShapeDtypeStruct(part_shape, BF16)),
            in_specs=[vmem] * 2,
            out_specs=(vmem,) * 2,
            compiler_params=params,
            name="pick",
        )(wanted, part)
    scaled, send = lax.optimization_barrier((0.9 * col_weight, send))
    other = lax.ppermute(send, "trans", swap)

    n_parts = 2
    updated, residual = pl.pallas_call(
        update_kernel,
        out_shape=(
            jax.ShapeDtypeStruct(volume.shape, F32),
            jax.ShapeDtypeStruct((own_rows, shared_views, det_cols), BF16),
        ),
        in_specs=[vmem] * 7,
        out_specs=(hbm, hbm),
        scratch_shapes=[
            pltpu.VMEM((n_wanted - slot_rows, det_cols), F32),
            pltpu.VMEM((n_seg * slot_rows, 2 * LANES), BF16),
            pltpu.VMEM(volume.shape, F32),
            pltpu.VMEM((own_rows, shared_views, det_cols), BF16),
            pltpu.SemaphoreType.DMA((n_parts,)),
            pltpu.SemaphoreType.DMA(()),
        ],
        compiler_params=params,
        name="update",
    )(volume, scaled, flat, windows, key, part, other)
    return updated, jnp.transpose(residual, (1, 0, 2))


def solution(mesh):
    in_specs = (
        P(("groups", "slab"), "trans"),
        P(("groups", "slab"), "trans"),
        P(None, "trans"),
        P(None, "trans"),
        P(("groups", "trans"), "slab", None),
        P(("groups", "trans"), "slab", None),
        P(("groups", "slab"), None, None),
        P(("groups", "slab")),
        P(("groups", "slab")),
        P(("groups", "slab")),
    )
    out_specs = (P(("groups", "slab"), "trans"), P(("groups", "trans"), "slab", None))
    return jax.shard_map(body, mesh=mesh, in_specs=in_specs, out_specs=out_specs, check_vma=False)
```

```python
import jax
import jax.numpy as jnp
from jax import lax
from jax.experimental import pallas as pl
from jax.experimental.pallas import tpu as pltpu
from jax.sharding import PartitionSpec as P

LANES = 128
WINDOW = 144
GROUP = 8
META = 8
F32 = jnp.float32
BF16 = jnp.bfloat16


def iota(shape, dim):
    return lax.broadcasted_iota(jnp.int32, shape, dim)


def segment_of(pos, width, n_seg):
    first = jnp.floor((pos - width - 0.5) * (1.0 / LANES))
    return jnp.clip(first, 0.0, n_seg - 1.0)


def slot_vector(values, repeat, index):
    result = jnp.full(index.shape, values[0], jnp.int32)
    for s in range(1, len(values)):
        result = jnp.where(index >= s * repeat, values[s], result)
    return result


def slot_lines(view_ref, block_ref, tile_rows, n_views, own_rows):
    lines = []
    for s in range(view_ref.shape[0]):
        for r in range(tile_rows):
            detector_row = block_ref[s] * tile_rows + r
            lines.append((detector_row // own_rows * n_views + view_ref[s]) * own_rows + detector_row % own_rows)
    return lines


def project_kernel(
    view_hbm, block_hbm, vol_hbm, pos_hbm, wid_hbm, meas_hbm, rw_hbm, tiles_hbm,
    own_ref, send_ref, win_ref, key_ref, flat_ref, across_ref, down_ref, vol_ref,
    view_ref, block_ref, pos_ref, wid_ref, meas_ref, rw_ref, tiles_ref, spread_ref, sems,
):
    inputs = (pos_hbm, wid_hbm, vol_hbm, view_hbm, block_hbm, tiles_hbm, meas_hbm, rw_hbm)
    holders = (pos_ref, wid_ref, vol_ref, view_ref, block_ref, tiles_ref, meas_ref, rw_ref)
    copies = [pltpu.make_async_copy(a, b, sems.at[i]) for i, (a, b) in enumerate(zip(inputs, holders))]
    for copy in copies:
        copy.start()
    n_views, cols = pos_ref.shape
    n_slots, tile_rows, _ = tiles_ref.shape
    shared_views, own_rows, det_cols = meas_ref.shape
    n_seg = det_cols // LANES
    slot_rows = n_slots * tile_rows
    own_lines = n_views * own_rows
    trans = lax.axis_index("trans")
    offsets = iota((WINDOW, cols), 0).astype(F32)
    copies[0].wait()
    copies[1].wait()
    segments = []
    for v in range(n_views):
        segments.append(segment_of(pos_ref[v : v + 1, :], wid_ref[v : v + 1, :], n_seg))

    def window(v):
        pos, wid = pos_ref[v : v + 1, :], wid_ref[v : v + 1, :]
        distance = jnp.abs(offsets + (segments[v] * LANES + 0.5 - pos)) * (1.0 / wid)
        win_ref[v] = jnp.maximum(0.0, 1.0 - distance).astype(BF16)

    first_views = n_views // 2
    for v in range(first_views):
        window(v)
    for copy in copies[3:]:
        copy.wait()
    tiles = tiles_ref[...].astype(F32)
    flat = jnp.concatenate([tiles[s, r : r + 1, :] for s in range(n_slots) for r in range(tile_rows)], axis=0)
    flat = flat.astype(BF16)
    flat_ref[...] = flat
    views = slot_vector([view_ref[s] for s in range(n_slots)], tile_rows, iota((slot_rows, cols), 0))
    key = jnp.broadcast_to(segments[0], (slot_rows, cols))
    for v in range(1, n_views):
        key = jnp.where(views == v, segments[v] + float(v * n_seg), key)
    key_ref[...] = key
    copies[2].wait()
    rows = jnp.dot(flat, vol_ref[...].astype(BF16), preferred_element_type=F32)
    sums = jnp.zeros((n_seg * slot_rows, WINDOW), F32)
    for v in range(n_views):
        for a in range(n_seg):
            spread_ref[v, a * slot_rows : (a + 1) * slot_rows, :] = jnp.where(key == v * n_seg + a, rows, 0.0).astype(BF16)
        if v >= first_views:
            window(v)
        sums = sums + lax.dot_general(
            spread_ref[v], win_ref[v], (((1,), (1,)), ((), ())), preferred_element_type=F32
        )
    numbers = slot_lines(view_ref, block_ref, tile_rows, n_views, own_rows)
    across_ref[...] = slot_vector(numbers, 1, iota(across_ref.shape, 1) & (slot_rows - 1))
    down_ref[...] = slot_vector(numbers, 1, iota(down_ref.shape, 0))
    lines = own_ref.shape[0] // n_seg - slot_rows
    place = iota((lines, det_cols), 0)
    block = jnp.zeros((lines, det_cols), F32)
    for i in range(shared_views):
        for j in range(own_rows):
            at = (trans * shared_views + i) * own_rows + j
            block = jnp.where(place == at, rw_ref[i, j : j + 1, :], block)
            block = jnp.where(place == own_lines + at, meas_ref[i, j : j + 1, :], block)
    for a in range(n_seg):
        at = n_seg * slot_rows + a * lines
        own_ref[at : at + lines, :] = block[:, a * LANES : (a + 1) * LANES]
    edge = WINDOW - LANES
    own_ref[: n_seg * slot_rows, :] = sums[:, :LANES]
    own_ref[slot_rows : n_seg * slot_rows, :edge] += sums[: (n_seg - 1) * slot_rows, LANES:]
    send_ref[...] = own_ref[...].astype(BF16)


def join_kernel(count_ref, across_ref, down_ref, own_ref, got_ref, out_ref, wanted_ref, *, tile_rows, own_lines):
    n_rows = own_ref.shape[0]
    slot_rows = down_ref.shape[0]
    out_ref[:n_rows, :] = (own_ref[...] + got_ref[...].astype(F32)).astype(BF16)
    shape = (META, LANES)
    live_rows = count_ref[0] * tile_rows
    live = (iota((1, LANES), 1) & (slot_rows - 1)) < live_rows
    line = jnp.where(live, across_ref[0:1, :], -1)
    part = jnp.where(iota(shape, 0) == 0, line & 127, line >> 7)
    out_ref[n_rows:, :] = part.astype(F32).astype(BF16)
    wanted_ref[:slot_rows, :] = jnp.where(iota((slot_rows, LANES), 0) < live_rows, down_ref[...], -2)
    shape = (wanted_ref.shape[0] - slot_rows, LANES)
    index = iota(shape, 0)
    wanted_ref[slot_rows:, :] = jnp.where(index < own_lines, lax.axis_index("slab") * own_lines + index, -2)


def gather_kernel(ids_ref, *refs, masks, slot_rows, own_lines, n_seg):
    payloads, (part_ref, send_ref, all_ref) = refs[:-3], refs[-3:]
    slab, trans = lax.axis_index("slab"), lax.axis_index("trans")
    depth = all_ref.shape[0]
    n_sources = len(payloads)
    block_lines = (payloads[0].shape[0] - META) // n_seg - slot_rows
    first_block = n_sources * slot_rows
    lane = iota((1, depth), 1)
    sum_line = jnp.full((1, depth), -1, jnp.int32)
    weight_line = sum_line
    if first_block + n_sources * block_lines < depth:
        used = first_block + n_sources * block_lines
        all_ref[used:, :] = jnp.zeros((depth - used, all_ref.shape[1]), F32)
    for j, ref in enumerate(payloads):
        values = ref[...].astype(F32)
        mask = jnp.where(trans == 0, masks[j][0], masks[j][1])
        taken = mask >= 0
        meta = values[n_seg * (slot_rows + block_lines) :]
        line = (meta[0:1, :] + 128.0 * meta[1:2, :]).astype(jnp.int32)
        line = jnp.concatenate([line] * (depth // LANES), axis=1)
        here = (lane >= j * slot_rows) & (lane < (j + 1) * slot_rows)
        sum_line = jnp.where(here & taken, line, sum_line)
        at = first_block + j * block_lines
        inside = lane - at
        base = (slab ^ mask) * own_lines
        weights = (inside >= 0) & (inside < own_lines) & taken
        weight_line = jnp.where(weights, base + inside, weight_line)
        measured = (inside >= own_lines) & (inside < 2 * own_lines) & taken
        sum_line = jnp.where(measured, base + inside - own_lines, sum_line)
        for a in range(n_seg):
            lanes = slice(a * LANES, (a + 1) * LANES)
            all_ref[j * slot_rows : (j + 1) * slot_rows, lanes] = values[a * slot_rows : (a + 1) * slot_rows]
            start = n_seg * slot_rows + a * block_lines
            all_ref[at : at + block_lines, lanes] = values[start : start + block_lines]
    ids = jnp.concatenate([ids_ref[...]] * (depth // LANES), axis=1)
    sign = jnp.where(lane >= first_block, -1.0, 1.0)
    chosen = jnp.concatenate(
        [jnp.where(ids == sum_line, sign, 0.0), jnp.where(ids == weight_line, 1.0, 0.0)], axis=0
    )
    part = jnp.dot(chosen.astype(BF16), all_ref[...].astype(BF16), preferred_element_type=F32)
    part_ref[...] = part
    send_ref[...] = part.astype(BF16)


def pick_kernel(ids_ref, part_ref, out_ref, send_ref):
    lines = part_ref.shape[0] // 2
    ids = jnp.concatenate([ids_ref[...]] * (-(-lines // LANES)), axis=1)[:, :lines]
    chosen = (iota(ids.shape, 1) == ids).astype(F32)
    for half in range(2):
        part = part_ref[half * lines : (half + 1) * lines, :]
        rows = slice(half * ids.shape[0], (half + 1) * ids.shape[0])
        picked = jnp.dot(chosen, part, preferred_element_type=F32, precision=lax.Precision.HIGHEST)
        out_ref[rows, :] = picked
        send_ref[rows, :] = picked.astype(BF16)


def update_kernel(
    vol_ref, cw_ref, flat_ref, win_ref, key_ref, part_ref, got_ref,
    upd_hbm, out_hbm,
    val_ref, near_ref, upd_ref, out_ref, sems, out_sem,
):
    n_views, _, cols = win_ref.shape
    own_rows, shared_views, det_cols = out_ref.shape
    n_seg = det_cols // LANES
    slot_rows = key_ref.shape[0]
    trans = lax.axis_index("trans")
    lines = part_ref.shape[0] // 2
    total = part_ref[...] + got_ref[...].astype(F32)
    residual = -total[:lines] * total[lines:]
    near = residual[:slot_rows].astype(BF16)
    val_ref[...] = residual[slot_rows:]
    for a in range(n_seg):
        at = slice(a * slot_rows, (a + 1) * slot_rows)
        near_ref[at, :LANES] = near[:, a * LANES : (a + 1) * LANES]
        if a + 1 < n_seg:
            near_ref[at, LANES:] = near[:, (a + 1) * LANES : (a + 2) * LANES]
        else:
            near_ref[at, LANES:] = jnp.zeros((slot_rows, LANES), BF16)
    copies = []
    n_parts = sems.shape[0]
    width = cols // n_parts
    spans = [slice(p * width, (p + 1) * width) for p in range(n_parts)]
    near_all = near_ref[:, :WINDOW]
    parts = [[jnp.dot(near_all, win_ref[v, :, at], preferred_element_type=F32) for v in range(n_views)] for at in spans]
    gradients = []
    for p, at in enumerate(spans):
        key = key_ref[:, at]
        back = jnp.zeros((slot_rows, width), F32)
        for v in range(n_views):
            for a in range(n_seg):
                back = jnp.where(key == v * n_seg + a, parts[p][v][a * slot_rows : (a + 1) * slot_rows], back)
        gradient = lax.dot_general(
            flat_ref[...], back.astype(BF16), (((0,), (0,)), ((), ())), preferred_element_type=F32
        )
        upd_ref[:, at] = vol_ref[:, at] + cw_ref[:, at] * gradient
        copies.append(pltpu.make_async_copy(upd_ref.at[:, at], upd_hbm.at[:, at], sems.at[p]))
        copies[-1].start()
    for i in range(shared_views):
        for j in range(own_rows):
            line = (trans * shared_views + i) * own_rows + j
            out_ref[j, i : i + 1, :] = val_ref[pl.ds(line, 1), :].astype(BF16)
    copies.append(pltpu.make_async_copy(out_ref, out_hbm, out_sem))
    copies[-1].start()
    for copy in copies:
        copy.wait()


def exchange(array, masks, n_slab):
    pairs = []
    for i in range(n_slab):
        for k, mask in enumerate(masks):
            pairs.append(((i ^ mask) * len(masks) + k, i * len(masks) + k))
    return lax.ppermute(array, ("slab", "trans"), pairs)


def direct_steps(n_group):
    half = n_group // 2
    near = [(mask, True) for mask in range(half, 0, -1)]
    far = [(1, False)] + [(mask, True) for mask in range(n_group - 1, half, -1)]
    if n_group == 8:
        near = [(mask, True) for mask in (4, 1, 3, 2)]
        far = [(1, False), (7, True), (5, True), (6, True)]
    return list(zip(near, far))


def body(
    volume, col_weight, foot_pos, foot_width, measured, row_weight, row_tiles, tile_view_index, tile_block, tile_count
):
    n_views, cols = foot_pos.shape
    shared_views, own_rows, det_cols = measured.shape
    n_slots, tile_rows, depth = row_tiles.shape
    n_slab, n_trans = lax.axis_size("slab"), lax.axis_size("trans")
    assert n_trans == 2 and n_slab & (n_slab - 1) == 0 and n_slab > 1
    assert LANES % (n_slots * tile_rows) == 0
    n_seg = det_cols // LANES
    slot_rows = n_slots * tile_rows
    own_lines = n_views * own_rows
    lines = n_slab * own_lines
    block_lines = -(-2 * own_lines // 8) * 8
    first_rows = n_seg * (slot_rows + block_lines)
    smem, vmem = pl.BlockSpec(memory_space=pltpu.SMEM), pl.BlockSpec(memory_space=pltpu.VMEM)
    hbm = pl.BlockSpec(memory_space=pltpu.HBM)
    params = pltpu.CompilerParams(vmem_limit_bytes=32 * 1024 * 1024)
    near = (tile_view_index, tile_block, volume, foot_pos, foot_width, measured, row_weight, row_tiles)
    own, send, windows, key, flat, across, down, held = pl.pallas_call(
        project_kernel,
        out_shape=(
            jax.ShapeDtypeStruct((first_rows, LANES), F32),
            jax.ShapeDtypeStruct((first_rows, LANES), BF16),
            jax.ShapeDtypeStruct((n_views, WINDOW, cols), BF16),
            jax.ShapeDtypeStruct((slot_rows, cols), F32),
            jax.ShapeDtypeStruct((slot_rows, depth), BF16),
            jax.ShapeDtypeStruct((8, LANES), jnp.int32),
            jax.ShapeDtypeStruct((slot_rows, LANES), jnp.int32),
            jax.ShapeDtypeStruct(volume.shape, F32),
        ),
        in_specs=[hbm] * 8,
        out_specs=(vmem,) * 8,
        scratch_shapes=[
            pltpu.SMEM(tile_view_index.shape, jnp.int32),
            pltpu.SMEM(tile_block.shape, jnp.int32),
            pltpu.VMEM(foot_pos.shape, F32),
            pltpu.VMEM(foot_width.shape, F32),
            pltpu.VMEM(measured.shape, F32),
            pltpu.VMEM(row_weight.shape, F32),
            pltpu.VMEM(row_tiles.shape, BF16),
            pltpu.VMEM((n_views, n_seg * slot_rows, cols), BF16),
            pltpu.SemaphoreType.DMA((8,)),
        ],
        compiler_params=params,
        name="project",
    )(*[pltpu.with_memory_space_constraint(array, pltpu.HBM) for array in near])

    swap = [(0, 1), (1, 0)]
    got = lax.ppermute(send, "trans", swap)
    tile_count, own = lax.optimization_barrier((tile_count, own))

    def join(*refs):
        join_kernel(*refs, tile_rows=tile_rows, own_lines=own_lines)

    n_wanted = slot_rows + -(-own_lines // 8) * 8
    payload, wanted = pl.pallas_call(
        join,
        out_shape=(
            jax.ShapeDtypeStruct((first_rows + META, LANES), BF16),
            jax.ShapeDtypeStruct((n_wanted, LANES), jnp.int32),
        ),
        in_specs=[smem] + [vmem] * 4,
        out_specs=(vmem,) * 2,
        compiler_params=params,
        name="join",
    )(tile_count, across, down, own, got)

    n_group = min(GROUP, n_slab)
    steps = direct_steps(n_group)
    arrived = [exchange(payload, [mask for mask, _ in step], n_slab) for step in steps]
    masks = [[mask if used else -1 for mask, used in step] for step in steps]

    def gather(*refs):
        gather_kernel(*refs, masks=[(-1, 0)] + masks, slot_rows=slot_rows, own_lines=own_lines, n_seg=n_seg)

    whole = n_group == n_slab
    ids = wanted if whole else jnp.broadcast_to(jnp.arange(lines, dtype=jnp.int32)[:, None], (lines, LANES))
    part_shape = (2 * ids.shape[0], det_cols)
    all_depth = -(-(1 + len(steps)) * (slot_rows + block_lines) // LANES) * LANES
    part, send = pl.pallas_call(
        gather,
        out_shape=(jax.ShapeDtypeStruct(part_shape, F32), jax.ShapeDtypeStruct(part_shape, BF16)),
        in_specs=[vmem] * (2 + len(steps)),
        out_specs=(vmem,) * 2,
        scratch_shapes=[pltpu.VMEM((all_depth, det_cols), F32)],
        compiler_params=params,
        name="gather",
    )(ids, payload, *arrived)
    if not whole:
        bit = n_group
        while bit < n_slab:
            part = part + exchange(part.astype(BF16), (bit, bit), n_slab).astype(F32)
            bit *= 2
        part_shape = (2 * n_wanted, det_cols)
        part, send = pl.pallas_call(
            pick_kernel,
            out_shape=(jax.ShapeDtypeStruct(part_shape, F32), jax.ShapeDtypeStruct(part_shape, BF16)),
            in_specs=[vmem] * 2,
            out_specs=(vmem,) * 2,
            compiler_params=params,
            name="pick",
        )(wanted, part)
    scaled, send = lax.optimization_barrier((0.9 * col_weight, send))
    other = lax.ppermute(send, "trans", swap)

    n_parts = 2
    updated, residual = pl.pallas_call(
        update_kernel,
        out_shape=(
            jax.ShapeDtypeStruct(volume.shape, F32),
            jax.ShapeDtypeStruct((own_rows, shared_views, det_cols), BF16),
        ),
        in_specs=[vmem] * 7,
        out_specs=(hbm, hbm),
        scratch_shapes=[
            pltpu.VMEM((n_wanted - slot_rows, det_cols), F32),
            pltpu.VMEM((n_seg * slot_rows, 2 * LANES), BF16),
            pltpu.VMEM(volume.shape, F32),
            pltpu.VMEM((own_rows, shared_views, det_cols), BF16),
            pltpu.SemaphoreType.DMA((n_parts,)),
            pltpu.SemaphoreType.DMA(()),
        ],
        compiler_params=params,
        name="update",
    )(held, scaled, flat, windows, key, part, other)
    return updated, jnp.transpose(residual, (1, 0, 2))


def solution(mesh):
    in_specs = (
        P(("groups", "slab"), "trans"),
        P(("groups", "slab"), "trans"),
        P(None, "trans"),
        P(None, "trans"),
        P(("groups", "trans"), "slab", None),
        P(("groups", "trans"), "slab", None),
        P(("groups", "slab"), None, None),
        P(("groups", "slab")),
        P(("groups", "slab")),
        P(("groups", "slab")),
    )
    out_specs = (P(("groups", "slab"), "trans"), P(("groups", "trans"), "slab", None))
    return jax.shard_map(body, mesh=mesh, in_specs=in_specs, out_specs=out_specs, check_vma=False)
```

```python
import jax
import jax.numpy as jnp
from jax import lax
from jax.experimental import pallas as pl
from jax.experimental.pallas import tpu as pltpu
from jax.sharding import PartitionSpec as P

LANES = 128
WINDOW = 144
GROUP = 8
META = 16
F32 = jnp.float32
BF16 = jnp.bfloat16


def iota(shape, dim):
    return lax.broadcasted_iota(jnp.int32, shape, dim)


def segment_of(pos, width, n_seg):
    first = jnp.floor((pos - width - 0.5) * (1.0 / LANES))
    return jnp.clip(first, 0.0, n_seg - 1.0)


def slot_vector(values, repeat, index):
    result = jnp.full(index.shape, values[0], jnp.int32)
    for s in range(1, len(values)):
        result = jnp.where(index >= s * repeat, values[s], result)
    return result


def slot_lines(view_ref, block_ref, tile_rows, n_views, own_rows):
    lines = []
    for s in range(view_ref.shape[0]):
        for r in range(tile_rows):
            detector_row = block_ref[s] * tile_rows + r
            lines.append((detector_row // own_rows * n_views + view_ref[s]) * own_rows + detector_row % own_rows)
    return lines


def project_kernel(
    view_hbm, block_hbm, vol_hbm, pos_hbm, wid_hbm, meas_hbm, rw_hbm, tiles_hbm,
    own_ref, send_ref, win_ref, key_ref, flat_ref, across_ref, down_ref, vol_ref,
    view_ref, block_ref, pos_ref, wid_ref, meas_ref, rw_ref, tiles_ref, spread_ref, sems,
):
    inputs = (pos_hbm, wid_hbm, vol_hbm, view_hbm, block_hbm, tiles_hbm, meas_hbm, rw_hbm)
    holders = (pos_ref, wid_ref, vol_ref, view_ref, block_ref, tiles_ref, meas_ref, rw_ref)
    copies = [pltpu.make_async_copy(a, b, sems.at[i]) for i, (a, b) in enumerate(zip(inputs, holders))]
    for copy in copies:
        copy.start()
    n_views, cols = pos_ref.shape
    n_slots, tile_rows, _ = tiles_ref.shape
    shared_views, own_rows, det_cols = meas_ref.shape
    n_seg = det_cols // LANES
    slot_rows = n_slots * tile_rows
    own_lines = n_views * own_rows
    trans = lax.axis_index("trans")
    offsets = iota((WINDOW, cols), 0).astype(F32)
    copies[0].wait()
    copies[1].wait()
    segments = []
    for v in range(n_views):
        segments.append(segment_of(pos_ref[v : v + 1, :], wid_ref[v : v + 1, :], n_seg))

    def window(v):
        pos, wid = pos_ref[v : v + 1, :], wid_ref[v : v + 1, :]
        distance = jnp.abs(offsets + (segments[v] * LANES + 0.5 - pos)) * (1.0 / wid)
        win_ref[v] = jnp.maximum(0.0, 1.0 - distance).astype(BF16)

    first_views = n_views // 2
    for v in range(first_views):
        window(v)
    for copy in copies[3:]:
        copy.wait()
    tiles = tiles_ref[...].astype(F32)
    flat = jnp.concatenate([tiles[s, r : r + 1, :] for s in range(n_slots) for r in range(tile_rows)], axis=0)
    flat = flat.astype(BF16)
    flat_ref[...] = flat
    views = slot_vector([view_ref[s] for s in range(n_slots)], tile_rows, iota((slot_rows, cols), 0))
    key = jnp.broadcast_to(segments[0], (slot_rows, cols))
    for v in range(1, n_views):
        key = jnp.where(views == v, segments[v] + float(v * n_seg), key)
    key_ref[...] = key
    copies[2].wait()
    rows = jnp.dot(flat, vol_ref[...].astype(BF16), preferred_element_type=F32)
    sums = jnp.zeros((n_seg * slot_rows, WINDOW), F32)
    for v in range(n_views):
        for a in range(n_seg):
            spread_ref[v, a * slot_rows : (a + 1) * slot_rows, :] = jnp.where(key == v * n_seg + a, rows, 0.0).astype(BF16)
        if v >= first_views:
            window(v)
        sums = sums + lax.dot_general(
            spread_ref[v], win_ref[v], (((1,), (1,)), ((), ())), preferred_element_type=F32
        )
    numbers = slot_lines(view_ref, block_ref, tile_rows, n_views, own_rows)
    across_ref[...] = slot_vector(numbers, 1, iota(across_ref.shape, 1) & (slot_rows - 1))
    down_ref[...] = slot_vector(numbers, 1, iota(down_ref.shape, 0))
    lines = own_ref.shape[0] // n_seg - slot_rows
    place = iota((lines, det_cols), 0)
    block = jnp.zeros((lines, det_cols), F32)
    for i in range(shared_views):
        for j in range(own_rows):
            at = (trans * shared_views + i) * own_rows + j
            block = jnp.where(place == at, rw_ref[i, j : j + 1, :], block)
            block = jnp.where(place == own_lines + at, meas_ref[i, j : j + 1, :], block)
    for a in range(n_seg):
        at = n_seg * slot_rows + a * lines
        own_ref[at : at + lines, :] = block[:, a * LANES : (a + 1) * LANES]
    edge = WINDOW - LANES
    own_ref[: n_seg * slot_rows, :] = sums[:, :LANES]
    own_ref[slot_rows : n_seg * slot_rows, :edge] += sums[: (n_seg - 1) * slot_rows, LANES:]
    send_ref[...] = own_ref[...].astype(BF16)


def join_kernel(count_ref, across_ref, down_ref, own_ref, got_ref, out_ref, wanted_ref, *, tile_rows, own_lines):
    n_rows = own_ref.shape[0]
    slot_rows = down_ref.shape[0]
    out_ref[:n_rows, :] = (own_ref[...] + got_ref[...].astype(F32)).astype(BF16)
    shape = (META, LANES)
    live_rows = count_ref[0] * tile_rows
    live = (iota((1, LANES), 1) & (slot_rows - 1)) < live_rows
    line = jnp.where(live, across_ref[0:1, :], -1)
    part = jnp.where(iota(shape, 0) == 0, line & 127, line >> 7)
    out_ref[n_rows:, :] = part.astype(F32).astype(BF16)
    wanted_ref[:slot_rows, :] = jnp.where(iota((slot_rows, LANES), 0) < live_rows, down_ref[...], -2)
    shape = (wanted_ref.shape[0] - slot_rows, LANES)
    index = iota(shape, 0)
    wanted_ref[slot_rows:, :] = jnp.where(index < own_lines, lax.axis_index("slab") * own_lines + index, -2)


def gather_kernel(ids_ref, *refs, masks, slot_rows, own_lines, n_seg):
    payloads, (part_ref, send_ref, all_ref) = refs[:-3], refs[-3:]
    slab, trans = lax.axis_index("slab"), lax.axis_index("trans")
    depth = all_ref.shape[0]
    n_sources = len(payloads)
    block_lines = (payloads[0].shape[0] - META) // n_seg - slot_rows
    first_block = n_sources * slot_rows
    lane = iota((1, depth), 1)
    sum_line = jnp.full((1, depth), -1, jnp.int32)
    weight_line = sum_line
    if first_block + n_sources * block_lines < depth:
        used = first_block + n_sources * block_lines
        all_ref[used:, :] = jnp.zeros((depth - used, all_ref.shape[1]), F32)
    for j, ref in enumerate(payloads):
        values = ref[...].astype(F32)
        mask = jnp.where(trans == 0, masks[j][0], masks[j][1])
        taken = mask >= 0
        meta = values[n_seg * (slot_rows + block_lines) :]
        line = (meta[0:1, :] + 128.0 * meta[1:2, :]).astype(jnp.int32)
        line = jnp.concatenate([line] * (depth // LANES), axis=1)
        here = (lane >= j * slot_rows) & (lane < (j + 1) * slot_rows)
        sum_line = jnp.where(here & taken, line, sum_line)
        at = first_block + j * block_lines
        inside = lane - at
        base = (slab ^ mask) * own_lines
        weights = (inside >= 0) & (inside < own_lines) & taken
        weight_line = jnp.where(weights, base + inside, weight_line)
        measured = (inside >= own_lines) & (inside < 2 * own_lines) & taken
        sum_line = jnp.where(measured, base + inside - own_lines, sum_line)
        for a in range(n_seg):
            lanes = slice(a * LANES, (a + 1) * LANES)
            all_ref[j * slot_rows : (j + 1) * slot_rows, lanes] = values[a * slot_rows : (a + 1) * slot_rows]
            start = n_seg * slot_rows + a * block_lines
            all_ref[at : at + block_lines, lanes] = values[start : start + block_lines]
    ids = jnp.concatenate([ids_ref[...]] * (depth // LANES), axis=1)
    sign = jnp.where(lane >= first_block, -1.0, 1.0)
    chosen = jnp.concatenate(
        [jnp.where(ids == sum_line, sign, 0.0), jnp.where(ids == weight_line, 1.0, 0.0)], axis=0
    )
    part = jnp.dot(chosen.astype(BF16), all_ref[...].astype(BF16), preferred_element_type=F32)
    part_ref[...] = part
    send_ref[...] = part.astype(BF16)


def pick_kernel(ids_ref, part_ref, out_ref, send_ref):
    lines = part_ref.shape[0] // 2
    ids = jnp.concatenate([ids_ref[...]] * (-(-lines // LANES)), axis=1)[:, :lines]
    chosen = (iota(ids.shape, 1) == ids).astype(F32)
    picked = []
    for half in range(2):
        part = part_ref[half * lines : (half + 1) * lines, :]
        picked.append(jnp.dot(chosen, part, preferred_element_type=F32, precision=lax.Precision.HIGHEST))
    out_ref[...] = jnp.concatenate(picked, axis=0)
    send_ref[...] = out_ref[...].astype(BF16)


def update_kernel(
    vol_ref, cw_ref, flat_ref, win_ref, key_ref, part_ref, got_ref,
    upd_hbm, out_hbm,
    val_ref, near_ref, upd_ref, out_ref, sems, out_sem,
):
    n_views, _, cols = win_ref.shape
    own_rows, shared_views, det_cols = out_ref.shape
    n_seg = det_cols // LANES
    slot_rows = key_ref.shape[0]
    trans = lax.axis_index("trans")
    lines = part_ref.shape[0] // 2
    total = part_ref[...] + got_ref[...].astype(F32)
    residual = -total[:lines] * total[lines:]
    near = residual[:slot_rows].astype(BF16)
    val_ref[...] = residual[slot_rows:]
    for a in range(n_seg):
        at = slice(a * slot_rows, (a + 1) * slot_rows)
        near_ref[at, :LANES] = near[:, a * LANES : (a + 1) * LANES]
        if a + 1 < n_seg:
            near_ref[at, LANES:] = near[:, (a + 1) * LANES : (a + 2) * LANES]
        else:
            near_ref[at, LANES:] = jnp.zeros((slot_rows, LANES), BF16)
    copies = []
    n_parts = sems.shape[0]
    width = cols // n_parts
    spans = [slice(p * width, (p + 1) * width) for p in range(n_parts)]
    near_all = near_ref[:, :WINDOW]
    parts = [[jnp.dot(near_all, win_ref[v, :, at], preferred_element_type=F32) for v in range(n_views)] for at in spans]
    gradients = []
    for p, at in enumerate(spans):
        key = key_ref[:, at]
        back = jnp.zeros((slot_rows, width), F32)
        for v in range(n_views):
            for a in range(n_seg):
                back = jnp.where(key == v * n_seg + a, parts[p][v][a * slot_rows : (a + 1) * slot_rows], back)
        gradient = lax.dot_general(
            flat_ref[...], back.astype(BF16), (((0,), (0,)), ((), ())), preferred_element_type=F32
        )
        upd_ref[:, at] = vol_ref[:, at] + cw_ref[:, at] * gradient
        copies.append(pltpu.make_async_copy(upd_ref.at[:, at], upd_hbm.at[:, at], sems.at[p]))
        copies[-1].start()
    for j in range(own_rows):
        own = [val_ref[pl.ds((trans * shared_views + i) * own_rows + j, 1), :] for i in range(shared_views)]
        out_ref[j] = jnp.concatenate(own, axis=0).astype(BF16)
    copies.append(pltpu.make_async_copy(out_ref, out_hbm, out_sem))
    copies[-1].start()
    for copy in copies:
        copy.wait()


def exchange(array, masks, n_slab):
    pairs = []
    for i in range(n_slab):
        for k, mask in enumerate(masks):
            pairs.append(((i ^ mask) * len(masks) + k, i * len(masks) + k))
    return lax.ppermute(array, ("slab", "trans"), pairs)


def direct_steps(n_group):
    half = n_group // 2
    near = [(mask, True) for mask in range(half, 0, -1)]
    far = [(1, False)] + [(mask, True) for mask in range(n_group - 1, half, -1)]
    if n_group == 8:
        near = [(mask, True) for mask in (4, 1, 3, 2)]
        far = [(1, False), (7, True), (5, True), (6, True)]
    return list(zip(near, far))


def body(
    volume, col_weight, foot_pos, foot_width, measured, row_weight, row_tiles, tile_view_index, tile_block, tile_count
):
    n_views, cols = foot_pos.shape
    shared_views, own_rows, det_cols = measured.shape
    n_slots, tile_rows, depth = row_tiles.shape
    n_slab, n_trans = lax.axis_size("slab"), lax.axis_size("trans")
    assert n_trans == 2 and n_slab & (n_slab - 1) == 0 and n_slab > 1
    assert LANES % (n_slots * tile_rows) == 0
    n_seg = det_cols // LANES
    slot_rows = n_slots * tile_rows
    own_lines = n_views * own_rows
    lines = n_slab * own_lines
    block_lines = -(-2 * own_lines // 8) * 8
    first_rows = n_seg * (slot_rows + block_lines)
    smem, vmem = pl.BlockSpec(memory_space=pltpu.SMEM), pl.BlockSpec(memory_space=pltpu.VMEM)
    hbm = pl.BlockSpec(memory_space=pltpu.HBM)
    params = pltpu.CompilerParams(vmem_limit_bytes=32 * 1024 * 1024)
    near = (tile_view_index, tile_block, volume, foot_pos, foot_width, measured, row_weight, row_tiles)
    own, send, windows, key, flat, across, down, held = pl.pallas_call(
        project_kernel,
        out_shape=(
            jax.ShapeDtypeStruct((first_rows, LANES), F32),
            jax.ShapeDtypeStruct((first_rows, LANES), BF16),
            jax.ShapeDtypeStruct((n_views, WINDOW, cols), BF16),
            jax.ShapeDtypeStruct((slot_rows, cols), F32),
            jax.ShapeDtypeStruct((slot_rows, depth), BF16),
            jax.ShapeDtypeStruct((8, LANES), jnp.int32),
            jax.ShapeDtypeStruct((slot_rows, LANES), jnp.int32),
            jax.ShapeDtypeStruct(volume.shape, F32),
        ),
        in_specs=[hbm] * 8,
        out_specs=(vmem,) * 8,
        scratch_shapes=[
            pltpu.SMEM(tile_view_index.shape, jnp.int32),
            pltpu.SMEM(tile_block.shape, jnp.int32),
            pltpu.VMEM(foot_pos.shape, F32),
            pltpu.VMEM(foot_width.shape, F32),
            pltpu.VMEM(measured.shape, F32),
            pltpu.VMEM(row_weight.shape, F32),
            pltpu.VMEM(row_tiles.shape, BF16),
            pltpu.VMEM((n_views, n_seg * slot_rows, cols), BF16),
            pltpu.SemaphoreType.DMA((8,)),
        ],
        compiler_params=params,
        name="project",
    )(*[pltpu.with_memory_space_constraint(array, pltpu.HBM) for array in near])

    swap = [(0, 1), (1, 0)]
    got = lax.ppermute(send, "trans", swap)
    tile_count, own = lax.optimization_barrier((tile_count, own))

    def join(*refs):
        join_kernel(*refs, tile_rows=tile_rows, own_lines=own_lines)

    n_wanted = slot_rows + -(-own_lines // 8) * 8
    payload, wanted = pl.pallas_call(
        join,
        out_shape=(
            jax.ShapeDtypeStruct((first_rows + META, LANES), BF16),
            jax.ShapeDtypeStruct((n_wanted, LANES), jnp.int32),
        ),
        in_specs=[smem] + [vmem] * 4,
        out_specs=(vmem,) * 2,
        compiler_params=params,
        name="join",
    )(tile_count, across, down, own, got)

    n_group = min(GROUP, n_slab)
    steps = direct_steps(n_group)
    arrived = [exchange(payload, [mask for mask, _ in step], n_slab) for step in steps]
    masks = [[mask if used else -1 for mask, used in step] for step in steps]

    def gather(*refs):
        gather_kernel(*refs, masks=[(-1, 0)] + masks, slot_rows=slot_rows, own_lines=own_lines, n_seg=n_seg)

    whole = n_group == n_slab
    ids = wanted if whole else jnp.broadcast_to(jnp.arange(lines, dtype=jnp.int32)[:, None], (lines, LANES))
    part_shape = (2 * ids.shape[0], det_cols)
    all_depth = -(-(1 + len(steps)) * (slot_rows + block_lines) // LANES) * LANES
    part, send = pl.pallas_call(
        gather,
        out_shape=(jax.ShapeDtypeStruct(part_shape, F32), jax.ShapeDtypeStruct(part_shape, BF16)),
        in_specs=[vmem] * (2 + len(steps)),
        out_specs=(vmem,) * 2,
        scratch_shapes=[pltpu.VMEM((all_depth, det_cols), F32)],
        compiler_params=params,
        name="gather",
    )(ids, payload, *arrived)
    if not whole:
        bit = n_group
        while bit < n_slab:
            part = part + exchange(part.astype(BF16), (bit, bit), n_slab).astype(F32)
            bit *= 2
        part_shape = (2 * n_wanted, det_cols)
        part, send = pl.pallas_call(
            pick_kernel,
            out_shape=(jax.ShapeDtypeStruct(part_shape, F32), jax.ShapeDtypeStruct(part_shape, BF16)),
            in_specs=[vmem] * 2,
            out_specs=(vmem,) * 2,
            compiler_params=params,
            name="pick",
        )(wanted, part)
    scaled, send = lax.optimization_barrier((0.9 * col_weight, send))
    other = lax.ppermute(send, "trans", swap)

    n_parts = 2
    updated, residual = pl.pallas_call(
        update_kernel,
        out_shape=(
            jax.ShapeDtypeStruct(volume.shape, F32),
            jax.ShapeDtypeStruct((own_rows, shared_views, det_cols), BF16),
        ),
        in_specs=[vmem] * 7,
        out_specs=(hbm, hbm),
        scratch_shapes=[
            pltpu.VMEM((n_wanted - slot_rows, det_cols), F32),
            pltpu.VMEM((n_seg * slot_rows, 2 * LANES), BF16),
            pltpu.VMEM(volume.shape, F32),
            pltpu.VMEM((own_rows, shared_views, det_cols), BF16),
            pltpu.SemaphoreType.DMA((n_parts,)),
            pltpu.SemaphoreType.DMA(()),
        ],
        compiler_params=params,
        name="update",
    )(held, scaled, flat, windows, key, part, other)
    return updated, jnp.transpose(residual, (1, 0, 2))


def solution(mesh):
    in_specs = (
        P(("groups", "slab"), "trans"),
        P(("groups", "slab"), "trans"),
        P(None, "trans"),
        P(None, "trans"),
        P(("groups", "trans"), "slab", None),
        P(("groups", "trans"), "slab", None),
        P(("groups", "slab"), None, None),
        P(("groups", "slab")),
        P(("groups", "slab")),
        P(("groups", "slab")),
    )
    out_specs = (P(("groups", "slab"), "trans"), P(("groups", "trans"), "slab", None))
    return jax.shard_map(body, mesh=mesh, in_specs=in_specs, out_specs=out_specs, check_vma=False)
```

```python
import jax
import jax.numpy as jnp
from jax import lax
from jax.experimental import pallas as pl
from jax.experimental.pallas import tpu as pltpu
from jax.sharding import PartitionSpec as P

LANES = 128
WINDOW = 144
GROUP = 8
META = 16
F32 = jnp.float32
BF16 = jnp.bfloat16


def iota(shape, dim):
    return lax.broadcasted_iota(jnp.int32, shape, dim)


def segment_of(pos, width, n_seg):
    first = jnp.floor((pos - width - 0.5) * (1.0 / LANES))
    return jnp.clip(first, 0.0, n_seg - 1.0)


def slot_vector(values, repeat, index):
    result = jnp.full(index.shape, values[0], jnp.int32)
    for s in range(1, len(values)):
        result = jnp.where(index >= s * repeat, values[s], result)
    return result


def slot_lines(view_ref, block_ref, tile_rows, n_views, own_rows):
    lines = []
    for s in range(view_ref.shape[0]):
        for r in range(tile_rows):
            detector_row = block_ref[s] * tile_rows + r
            lines.append((detector_row // own_rows * n_views + view_ref[s]) * own_rows + detector_row % own_rows)
    return lines


def project_kernel(
    view_hbm, block_hbm, vol_hbm, pos_hbm, wid_hbm, meas_hbm, rw_hbm, tiles_hbm,
    own_ref, send_ref, win_ref, key_ref, flat_ref, across_ref, down_ref, vol_ref,
    view_ref, block_ref, pos_ref, wid_ref, meas_ref, rw_ref, tiles_ref, spread_ref, sems,
):
    inputs = (pos_hbm, wid_hbm, vol_hbm, view_hbm, block_hbm, tiles_hbm, meas_hbm, rw_hbm)
    holders = (pos_ref, wid_ref, vol_ref, view_ref, block_ref, tiles_ref, meas_ref, rw_ref)
    copies = [pltpu.make_async_copy(a, b, sems.at[i]) for i, (a, b) in enumerate(zip(inputs, holders))]
    for copy in copies:
        copy.start()
    n_views, cols = pos_ref.shape
    n_slots, tile_rows, _ = tiles_ref.shape
    shared_views, own_rows, det_cols = meas_ref.shape
    n_seg = det_cols // LANES
    slot_rows = n_slots * tile_rows
    own_lines = n_views * own_rows
    trans = lax.axis_index("trans")
    offsets = iota((WINDOW, cols), 0).astype(F32)
    copies[0].wait()
    copies[1].wait()
    segments = []
    for v in range(n_views):
        segments.append(segment_of(pos_ref[v : v + 1, :], wid_ref[v : v + 1, :], n_seg))

    def window(v):
        pos, wid = pos_ref[v : v + 1, :], wid_ref[v : v + 1, :]
        distance = jnp.abs(offsets + (segments[v] * LANES + 0.5 - pos)) * (1.0 / wid)
        win_ref[v] = jnp.maximum(0.0, 1.0 - distance).astype(BF16)

    first_views = n_views // 2
    for v in range(first_views):
        window(v)
    for copy in copies[3:]:
        copy.wait()
    tiles = tiles_ref[...].astype(F32)
    flat = jnp.concatenate([tiles[s, r : r + 1, :] for s in range(n_slots) for r in range(tile_rows)], axis=0)
    flat = flat.astype(BF16)
    flat_ref[...] = flat
    views = slot_vector([view_ref[s] for s in range(n_slots)], tile_rows, iota((slot_rows, cols), 0))
    key = jnp.broadcast_to(segments[0], (slot_rows, cols))
    for v in range(1, n_views):
        key = jnp.where(views == v, segments[v] + float(v * n_seg), key)
    key_ref[...] = key
    numbers = slot_lines(view_ref, block_ref, tile_rows, n_views, own_rows)
    across_ref[...] = slot_vector(numbers, 1, iota(across_ref.shape, 1) & (slot_rows - 1))
    down_ref[...] = slot_vector(numbers, 1, iota(down_ref.shape, 0))
    lines = own_ref.shape[0] // n_seg - slot_rows
    place = iota((lines, det_cols), 0)
    block = jnp.zeros((lines, det_cols), F32)
    for i in range(shared_views):
        for j in range(own_rows):
            at = (trans * shared_views + i) * own_rows + j
            block = jnp.where(place == at, rw_ref[i, j : j + 1, :], block)
            block = jnp.where(place == own_lines + at, meas_ref[i, j : j + 1, :], block)
    for a in range(n_seg):
        at = n_seg * slot_rows + a * lines
        own_ref[at : at + lines, :] = block[:, a * LANES : (a + 1) * LANES]
    copies[2].wait()
    rows = jnp.dot(flat, vol_ref[...].astype(BF16), preferred_element_type=F32)
    sums = jnp.zeros((n_seg * slot_rows, WINDOW), F32)
    for v in range(n_views):
        for a in range(n_seg):
            spread_ref[v, a * slot_rows : (a + 1) * slot_rows, :] = jnp.where(key == v * n_seg + a, rows, 0.0).astype(BF16)
        if v >= first_views:
            window(v)
        sums = sums + lax.dot_general(
            spread_ref[v], win_ref[v], (((1,), (1,)), ((), ())), preferred_element_type=F32
        )
    edge = WINDOW - LANES
    own_ref[: n_seg * slot_rows, :] = sums[:, :LANES]
    own_ref[slot_rows : n_seg * slot_rows, :edge] += sums[: (n_seg - 1) * slot_rows, LANES:]
    send_ref[...] = own_ref[...].astype(BF16)


def join_kernel(count_ref, across_ref, down_ref, own_ref, got_ref, out_ref, wanted_ref, *, tile_rows, own_lines):
    n_rows = own_ref.shape[0]
    slot_rows = down_ref.shape[0]
    out_ref[:n_rows, :] = (own_ref[...] + got_ref[...].astype(F32)).astype(BF16)
    shape = (META, LANES)
    live_rows = count_ref[0] * tile_rows
    live = (iota((1, LANES), 1) & (slot_rows - 1)) < live_rows
    line = jnp.where(live, across_ref[0:1, :], -1)
    part = jnp.where(iota(shape, 0) == 0, line & 127, line >> 7)
    out_ref[n_rows:, :] = part.astype(F32).astype(BF16)
    wanted_ref[:slot_rows, :] = jnp.where(iota((slot_rows, LANES), 0) < live_rows, down_ref[...], -2)
    shape = (wanted_ref.shape[0] - slot_rows, LANES)
    index = iota(shape, 0)
    wanted_ref[slot_rows:, :] = jnp.where(index < own_lines, lax.axis_index("slab") * own_lines + index, -2)


def gather_kernel(ids_ref, *refs, masks, slot_rows, own_lines, n_seg):
    payloads, (part_ref, send_ref, all_ref) = refs[:-3], refs[-3:]
    slab, trans = lax.axis_index("slab"), lax.axis_index("trans")
    depth = all_ref.shape[0]
    n_sources = len(payloads)
    block_lines = (payloads[0].shape[0] - META) // n_seg - slot_rows
    first_block = n_sources * slot_rows
    lane = iota((1, depth), 1)
    sum_line = jnp.full((1, depth), -1, jnp.int32)
    weight_line = sum_line
    if first_block + n_sources * block_lines < depth:
        used = first_block + n_sources * block_lines
        all_ref[used:, :] = jnp.zeros((depth - used, all_ref.shape[1]), F32)
    for j, ref in enumerate(payloads):
        values = ref[...].astype(F32)
        mask = jnp.where(trans == 0, masks[j][0], masks[j][1])
        taken = mask >= 0
        meta = values[n_seg * (slot_rows + block_lines) :]
        line = (meta[0:1, :] + 128.0 * meta[1:2, :]).astype(jnp.int32)
        line = jnp.concatenate([line] * (depth // LANES), axis=1)
        here = (lane >= j * slot_rows) & (lane < (j + 1) * slot_rows)
        sum_line = jnp.where(here & taken, line, sum_line)
        at = first_block + j * block_lines
        inside = lane - at
        base = (slab ^ mask) * own_lines
        weights = (inside >= 0) & (inside < own_lines) & taken
        weight_line = jnp.where(weights, base + inside, weight_line)
        measured = (inside >= own_lines) & (inside < 2 * own_lines) & taken
        sum_line = jnp.where(measured, base + inside - own_lines, sum_line)
        for a in range(n_seg):
            lanes = slice(a * LANES, (a + 1) * LANES)
            all_ref[j * slot_rows : (j + 1) * slot_rows, lanes] = values[a * slot_rows : (a + 1) * slot_rows]
            start = n_seg * slot_rows + a * block_lines
            all_ref[at : at + block_lines, lanes] = values[start : start + block_lines]
    ids = jnp.concatenate([ids_ref[...]] * (depth // LANES), axis=1)
    sign = jnp.where(lane >= first_block, -1.0, 1.0)
    chosen = jnp.concatenate(
        [jnp.where(ids == sum_line, sign, 0.0), jnp.where(ids == weight_line, 1.0, 0.0)], axis=0
    )
    part = jnp.dot(chosen.astype(BF16), all_ref[...].astype(BF16), preferred_element_type=F32)
    part_ref[...] = part
    send_ref[...] = part.astype(BF16)


def pick_kernel(ids_ref, part_ref, out_ref, send_ref):
    lines = part_ref.shape[0] // 2
    ids = jnp.concatenate([ids_ref[...]] * (-(-lines // LANES)), axis=1)[:, :lines]
    chosen = (iota(ids.shape, 1) == ids).astype(F32)
    picked = []
    for half in range(2):
        part = part_ref[half * lines : (half + 1) * lines, :]
        picked.append(jnp.dot(chosen, part, preferred_element_type=F32, precision=lax.Precision.HIGHEST))
    out_ref[...] = jnp.concatenate(picked, axis=0)
    send_ref[...] = out_ref[...].astype(BF16)


def update_kernel(
    vol_ref, cw_ref, flat_ref, win_ref, key_ref, part_ref, got_ref,
    upd_hbm, out_hbm,
    val_ref, near_ref, upd_ref, out_ref, sems, out_sem,
):
    n_views, _, cols = win_ref.shape
    own_rows, shared_views, det_cols = out_ref.shape
    n_seg = det_cols // LANES
    slot_rows = key_ref.shape[0]
    trans = lax.axis_index("trans")
    lines = part_ref.shape[0] // 2
    total = part_ref[...] + got_ref[...].astype(F32)
    residual = -total[:lines] * total[lines:]
    near = residual[:slot_rows].astype(BF16)
    val_ref[...] = residual[slot_rows:]
    for a in range(n_seg):
        at = slice(a * slot_rows, (a + 1) * slot_rows)
        near_ref[at, :LANES] = near[:, a * LANES : (a + 1) * LANES]
        if a + 1 < n_seg:
            near_ref[at, LANES:] = near[:, (a + 1) * LANES : (a + 2) * LANES]
        else:
            near_ref[at, LANES:] = jnp.zeros((slot_rows, LANES), BF16)
    copies = []
    n_parts = sems.shape[0]
    width = cols // n_parts
    spans = [slice(p * width, (p + 1) * width) for p in range(n_parts)]
    near_all = near_ref[:, :WINDOW]
    parts = [[jnp.dot(near_all, win_ref[v, :, at], preferred_element_type=F32) for v in range(n_views)] for at in spans]
    gradients = []
    for p, at in enumerate(spans):
        key = key_ref[:, at]
        back = jnp.zeros((slot_rows, width), F32)
        for v in range(n_views):
            for a in range(n_seg):
                back = jnp.where(key == v * n_seg + a, parts[p][v][a * slot_rows : (a + 1) * slot_rows], back)
        gradient = lax.dot_general(
            flat_ref[...], back.astype(BF16), (((0,), (0,)), ((), ())), preferred_element_type=F32
        )
        upd_ref[:, at] = vol_ref[:, at] + cw_ref[:, at] * gradient
        copies.append(pltpu.make_async_copy(upd_ref.at[:, at], upd_hbm.at[:, at], sems.at[p]))
        copies[-1].start()
    for j in range(own_rows):
        own = [val_ref[pl.ds((trans * shared_views + i) * own_rows + j, 1), :] for i in range(shared_views)]
        out_ref[j] = jnp.concatenate(own, axis=0).astype(BF16)
    copies.append(pltpu.make_async_copy(out_ref, out_hbm, out_sem))
    copies[-1].start()
    for copy in copies:
        copy.wait()


def exchange(array, masks, n_slab):
    pairs = []
    for i in range(n_slab):
        for k, mask in enumerate(masks):
            pairs.append(((i ^ mask) * len(masks) + k, i * len(masks) + k))
    return lax.ppermute(array, ("slab", "trans"), pairs)


def direct_steps(n_group):
    half = n_group // 2
    near = [(mask, True) for mask in range(half, 0, -1)]
    far = [(1, False)] + [(mask, True) for mask in range(n_group - 1, half, -1)]
    if n_group == 8:
        near = [(mask, True) for mask in (4, 1, 3, 2)]
        far = [(1, False), (7, True), (5, True), (6, True)]
    return list(zip(near, far))


def body(
    volume, col_weight, foot_pos, foot_width, measured, row_weight, row_tiles, tile_view_index, tile_block, tile_count
):
    n_views, cols = foot_pos.shape
    shared_views, own_rows, det_cols = measured.shape
    n_slots, tile_rows, depth = row_tiles.shape
    n_slab, n_trans = lax.axis_size("slab"), lax.axis_size("trans")
    assert n_trans == 2 and n_slab & (n_slab - 1) == 0 and n_slab > 1
    assert LANES % (n_slots * tile_rows) == 0
    n_seg = det_cols // LANES
    slot_rows = n_slots * tile_rows
    own_lines = n_views * own_rows
    lines = n_slab * own_lines
    block_lines = -(-2 * own_lines // 8) * 8
    first_rows = n_seg * (slot_rows + block_lines)
    smem, vmem = pl.BlockSpec(memory_space=pltpu.SMEM), pl.BlockSpec(memory_space=pltpu.VMEM)
    hbm = pl.BlockSpec(memory_space=pltpu.HBM)
    params = pltpu.CompilerParams(vmem_limit_bytes=32 * 1024 * 1024)
    near = (tile_view_index, tile_block, volume, foot_pos, foot_width, measured, row_weight, row_tiles)
    own, send, windows, key, flat, across, down, held = pl.pallas_call(
        project_kernel,
        out_shape=(
            jax.ShapeDtypeStruct((first_rows, LANES), F32),
            jax.ShapeDtypeStruct((first_rows, LANES), BF16),
            jax.ShapeDtypeStruct((n_views, WINDOW, cols), BF16),
            jax.ShapeDtypeStruct((slot_rows, cols), F32),
            jax.ShapeDtypeStruct((slot_rows, depth), BF16),
            jax.ShapeDtypeStruct((8, LANES), jnp.int32),
            jax.ShapeDtypeStruct((slot_rows, LANES), jnp.int32),
            jax.ShapeDtypeStruct(volume.shape, F32),
        ),
        in_specs=[hbm] * 8,
        out_specs=(vmem,) * 8,
        scratch_shapes=[
            pltpu.SMEM(tile_view_index.shape, jnp.int32),
            pltpu.SMEM(tile_block.shape, jnp.int32),
            pltpu.VMEM(foot_pos.shape, F32),
            pltpu.VMEM(foot_width.shape, F32),
            pltpu.VMEM(measured.shape, F32),
            pltpu.VMEM(row_weight.shape, F32),
            pltpu.VMEM(row_tiles.shape, BF16),
            pltpu.VMEM((n_views, n_seg * slot_rows, cols), BF16),
            pltpu.SemaphoreType.DMA((8,)),
        ],
        compiler_params=params,
        name="project",
    )(*[pltpu.with_memory_space_constraint(array, pltpu.HBM) for array in near])

    swap = [(0, 1), (1, 0)]
    got = lax.ppermute(send, "trans", swap)
    tile_count, own = lax.optimization_barrier((tile_count, own))

    def join(*refs):
        join_kernel(*refs, tile_rows=tile_rows, own_lines=own_lines)

    n_wanted = slot_rows + -(-own_lines // 8) * 8
    payload, wanted = pl.pallas_call(
        join,
        out_shape=(
            jax.ShapeDtypeStruct((first_rows + META, LANES), BF16),
            jax.ShapeDtypeStruct((n_wanted, LANES), jnp.int32),
        ),
        in_specs=[smem] + [vmem] * 4,
        out_specs=(vmem,) * 2,
        compiler_params=params,
        name="join",
    )(tile_count, across, down, own, got)

    n_group = min(GROUP, n_slab)
    steps = direct_steps(n_group)
    arrived = [exchange(payload, [mask for mask, _ in step], n_slab) for step in steps]
    masks = [[mask if used else -1 for mask, used in step] for step in steps]

    def gather(*refs):
        gather_kernel(*refs, masks=[(-1, 0)] + masks, slot_rows=slot_rows, own_lines=own_lines, n_seg=n_seg)

    whole = n_group == n_slab
    ids = wanted if whole else jnp.broadcast_to(jnp.arange(lines, dtype=jnp.int32)[:, None], (lines, LANES))
    part_shape = (2 * ids.shape[0], det_cols)
    all_depth = -(-(1 + len(steps)) * (slot_rows + block_lines) // LANES) * LANES
    part, send = pl.pallas_call(
        gather,
        out_shape=(jax.ShapeDtypeStruct(part_shape, F32), jax.ShapeDtypeStruct(part_shape, BF16)),
        in_specs=[vmem] * (2 + len(steps)),
        out_specs=(vmem,) * 2,
        scratch_shapes=[pltpu.VMEM((all_depth, det_cols), F32)],
        compiler_params=params,
        name="gather",
    )(ids, payload, *arrived)
    if not whole:
        bit = n_group
        while bit < n_slab:
            part = part + exchange(part.astype(BF16), (bit, bit), n_slab).astype(F32)
            bit *= 2
        part_shape = (2 * n_wanted, det_cols)
        part, send = pl.pallas_call(
            pick_kernel,
            out_shape=(jax.ShapeDtypeStruct(part_shape, F32), jax.ShapeDtypeStruct(part_shape, BF16)),
            in_specs=[vmem] * 2,
            out_specs=(vmem,) * 2,
            compiler_params=params,
            name="pick",
        )(wanted, part)
    scaled, send = lax.optimization_barrier((0.9 * col_weight, send))
    other = lax.ppermute(send, "trans", swap)

    n_parts = 2
    updated, residual = pl.pallas_call(
        update_kernel,
        out_shape=(
            jax.ShapeDtypeStruct(volume.shape, F32),
            jax.ShapeDtypeStruct((own_rows, shared_views, det_cols), BF16),
        ),
        in_specs=[vmem] * 7,
        out_specs=(hbm, hbm),
        scratch_shapes=[
            pltpu.VMEM((n_wanted - slot_rows, det_cols), F32),
            pltpu.VMEM((n_seg * slot_rows, 2 * LANES), BF16),
            pltpu.VMEM(volume.shape, F32),
            pltpu.VMEM((own_rows, shared_views, det_cols), BF16),
            pltpu.SemaphoreType.DMA((n_parts,)),
            pltpu.SemaphoreType.DMA(()),
        ],
        compiler_params=params,
        name="update",
    )(held, scaled, flat, windows, key, part, other)
    return updated, jnp.transpose(residual, (1, 0, 2))


def solution(mesh):
    in_specs = (
        P(("groups", "slab"), "trans"),
        P(("groups", "slab"), "trans"),
        P(None, "trans"),
        P(None, "trans"),
        P(("groups", "trans"), "slab", None),
        P(("groups", "trans"), "slab", None),
        P(("groups", "slab"), None, None),
        P(("groups", "slab")),
        P(("groups", "slab")),
        P(("groups", "slab")),
    )
    out_specs = (P(("groups", "slab"), "trans"), P(("groups", "trans"), "slab", None))
    return jax.shard_map(body, mesh=mesh, in_specs=in_specs, out_specs=out_specs, check_vma=False)
```
